512 devices in a mesh: grid: 64 (over z, y), rep: 8 (over x, core).
Axes of the slice: x: 4, y: 8, z: 8, core: 2. Of those that a mesh axis runs over, the one named last changes fastest.
Arguments:
- b_tensor: bfloat16 [8, 1024, 8192], P('rep', 'grid'), may hold values from -6 to 6
- green_occ: bfloat16 [8, 1024, 1024], P('rep', 'grid'), may hold values from -0.1875 to 0.1875
- green_vir: bfloat16 [8, 1024, 1024], P('rep', 'grid'), may hold values from -0.1875 to 0.1875
- b_pattern: int32 [8, 16, 16], P('rep'), may hold values 0 or 1
- g_pattern: int32 [8, 16, 16], P('rep'), may hold values 0 or 1
Outputs:
- occ_tensor: bfloat16 [8, 1024, 8192], P('rep', None, 'grid')
- vir_tensor: bfloat16 [8, 1024, 8192], P('rep', 'grid')
- chi: float32 [8, 8], replicated
The draws below stay inside these ranges and needn't reach their ends.
All inputs are finite; a program needn't handle non-finite values. No bound on the sum of `b_pattern` or of `g_pattern` on one device may be relied on, other than what follows from the above.
Results may differ from the reference program's by a relative error of at most 0.0056.
Values may be sent and summed in bfloat16 or wider, within the bound.
A program may use at most 64 MiB of HBM per device.

```python
import math
import jax
import jax.numpy as jnp
from jax import lax

BS = 64
MOLS = 16
RB = 8
DA = 1024
PAIRS = 8


def touch_ends(entries, rng, least, largest):
    extent = entries.shape
    place = [jax.random.randint(jax.random.fold_in(rng, axis), (), 0, extent[axis]) for axis in range(len(extent))]
    entries = entries.at[tuple(place)].set(least)
    longest = extent.index(max(extent))
    place[longest] = (place[longest] + 1) % extent[longest]
    return entries.at[tuple(place)].set(largest)


def levels(key, extent, split, smallest, high):
    gain, own = 1.0, jax.random.fold_in(key, 6)
    for axis_at, blocks in split:
        heights = jnp.exp(jax.random.uniform(jax.random.fold_in(own, axis_at), (blocks,), jnp.float32, smallest / len(split), high / len(split)))
        gain = gain * jnp.repeat(heights, extent[axis_at] // blocks).reshape([-1 if axis == axis_at else 1 for axis in range(len(extent))])
    return gain


def normal_values(own_key, shape, width, reach, shards=(), kind=jnp.bfloat16):
    drawn = jax.random.normal(own_key, shape, jnp.float32) * width
    if len(shards) > 0:
        drawn = levels(own_key, shape, shards, -0.22, 0.18) * drawn
    return jnp.clip(drawn, min=-reach, max=reach).astype(kind)


def setup_inputs(seed: int = 0) -> dict:
    streams_of = jax.random.split(jax.random.key(seed), 6)
    b_tensor = normal_values(streams_of[0], (PAIRS, DA, DA * RB), 1.0, 6.0, ((0, 8), (1, 64)))
    green_occ = normal_values(streams_of[1], (PAIRS, DA, DA), DA ** -0.5, 0.1875, ((0, 8), (1, 64)))
    green_vir = normal_values(streams_of[2], (PAIRS, DA, DA), DA ** -0.5, 0.1875, ((0, 8), (1, 64)))
    b_pattern = touch_ends((jax.random.randint(streams_of[3], (PAIRS, MOLS, MOLS), 0, 4) < 3).astype(jnp.int32), jax.random.fold_in(streams_of[3], 1), 0, 1)
    g_pattern = touch_ends((jax.random.randint(streams_of[4], (PAIRS, MOLS, MOLS), 0, 4) < 3).astype(jnp.int32), jax.random.fold_in(streams_of[4], 1), 0, 1)
    return {"b_tensor": b_tensor, "green_occ": green_occ, "green_vir": green_vir, "b_pattern": b_pattern, "g_pattern": g_pattern}


def expand(pattern):
    return jnp.repeat(jnp.repeat(pattern, BS, axis=0), BS, axis=1)

def one_pair(operands):
    tensor, occ_green, vir_green, tensor_pattern, green_pattern = operands
    tensor = tensor.reshape(DA, DA, RB)
    blocks = tensor * expand(tensor_pattern).astype(jnp.bfloat16)[:, :, None]
    green_mask = expand(green_pattern).astype(jnp.bfloat16)
    occ = occ_green * green_mask
    vir = vir_green * green_mask
    blocks_wide = blocks.astype(jnp.float32)
    occ_part = jnp.einsum('lm,mnp->lnp', occ.astype(jnp.float32), blocks_wide).astype(jnp.bfloat16)
    vir_part = jnp.einsum('lsq,sn->lnq', blocks_wide, vir.astype(jnp.float32)).astype(jnp.bfloat16)
    chi_part = jnp.einsum('lnp,lnq->pq', occ_part.astype(jnp.float32), vir_part.astype(jnp.float32))
    return (occ_part.reshape(DA, DA * RB), vir_part.reshape(DA, DA * RB), chi_part)

def reference(b_tensor, green_occ, green_vir, b_pattern, g_pattern):
    occ_tensor, vir_tensor, partials = lax.map(one_pair, (b_tensor, green_occ, green_vir, b_pattern, g_pattern))
    scale = -1.0 / (DA * math.sqrt(PAIRS))
    chi = lax.optimization_barrier(jnp.sum(partials, axis=0)) * scale
    return (occ_tensor, vir_tensor, chi)
```

```python
import functools
import math

import jax
import jax.numpy as jnp
from jax import lax
from jax.experimental import pallas as pl
from jax.experimental.pallas import tpu as pltpu
from jax.sharding import PartitionSpec as P

MESH = pl.DeviceIdType.MESH
SIDE = 8
ROWS = 16
ORBS = 1024
RB = 8
TILE = ROWS * RB
WIDE = SIDE * TILE
CHUNK = SIDE * ROWS
HALF = CHUNK // 2
ITEMS = 7
F32 = jnp.float32
BF16 = jnp.bfloat16


def around(index, step):
    return lax.rem(index + (step + SIDE), SIDE)


def kernel(
    scale,
    b_ref,
    occ_ref,
    vir_ref,
    bp_ref,
    gp_ref,
    occ_out,
    vir_out,
    chi_out,
    green,
    spread,
    middle,
    landed,
    columns,
    perm,
    left_side,
    total,
    mixed,
    shares,
    one_send,
    one_recv,
    ring_send,
    ring_recv,
    swap_send,
    swap_recv,
    chi_send,
    chi_recv,
):
    grid_ix = lax.axis_index("grid")
    rep_ix = lax.axis_index("rep")
    z, y = grid_ix // SIDE, grid_ix % SIDE
    core = rep_ix % 2
    a0 = z + core * (y - z)
    b0 = y + core * (z - y)
    sa = SIDE - (SIDE - 1) * core
    sb = 1 + (SIDE - 1) * core

    def nat(a, b):
        return a * sa + b * sb

    def at(a, b):
        return (nat(a, b), rep_ix)

    def remote(src, dst, send, recv, where):
        return pltpu.make_async_remote_copy(
            src_ref=src, dst_ref=dst, send_sem=send, recv_sem=recv, device_id=where, device_id_type=MESH
        )

    barrier = pltpu.get_barrier_semaphore()

    def greet(i, carry):
        for where in (at(around(a0, i), b0), at(a0, around(b0, i)), (grid_ix, around(rep_ix, i))):
            pl.semaphore_signal(barrier, inc=1, device_id=where, device_id_type=MESH)
        return carry

    lax.fori_loop(1, SIDE, greet, 0)

    molecule = grid_ix // 4
    lane = lax.broadcasted_iota(jnp.int32, (ROWS, 128), 1)
    me = a0 * SIDE + b0
    for t in range(SIDE):
        lo = gp_ref[0, molecule, 2 * t]
        hi = gp_ref[0, molecule, 2 * t + 1]
        keep = jnp.where(lane < 64, lo, hi).astype(F32).astype(BF16)
        cols = slice(t * 128, (t + 1) * 128)
        green[0, me, :, cols] = vir_ref[0, :, cols] * keep
        green[1, me, :, cols] = occ_ref[0, :, cols] * keep

    def lay(a, carry):
        for b in range(SIDE):
            n = nat(a, b)
            keep = jnp.full((ROWS, TILE), bp_ref[0, molecule, n // 4], jnp.int32).astype(F32).astype(BF16)
            tile = b_ref[0, :, pl.ds(pl.multiple_of(n * TILE, TILE), TILE)]
            spread[0, a, :, b * TILE : (b + 1) * TILE] = tile * keep
        return carry

    lax.fori_loop(0, SIDE, lay, 0)

    pl.semaphore_wait(barrier, 3 * (SIDE - 1))

    def first(which):
        def body(i, carry):
            block = green.at[which, me]
            remote(block, block, one_send.at[which], one_recv.at[which], at(a0, around(b0, i))).start()
            return carry

        lax.fori_loop(1, SIDE, body, 0)

    def first_done(which):
        seven = green.at[which, pl.ds(0, SIDE - 1)]
        remote(seven, seven, one_send.at[which], one_recv.at[which], at(a0, around(b0, 1))).wait()

    def swap_a(which):
        def body(i, carry):
            a = around(a0, i)
            remote(
                spread.at[which, a],
                middle.at[which, a0],
                swap_send.at[which, 0],
                swap_recv.at[which, 0],
                at(a, b0),
            ).start()
            return carry

        lax.fori_loop(1, SIDE, body, 0)
        middle[which, a0] = spread[which, a0]

    def swap_a_done(which):
        seven = middle.at[which, pl.ds(0, SIDE - 1)]
        remote(seven, seven, swap_send.at[which, 0], swap_recv.at[which, 0], at(around(a0, 1), b0)).wait()

    def tile_of(b):
        return pl.ds(pl.multiple_of(b * TILE, TILE), TILE)

    def swap_b(which):
        def body(i, carry):
            b = around(b0, i)
            remote(
                middle.at[which, :, :, tile_of(b)],
                landed.at[which, b0],
                swap_send.at[which, 1],
                swap_recv.at[which, 1],
                at(a0, b),
            ).start()
            return carry

        lax.fori_loop(1, SIDE, body, 0)
        landed[which, b0] = middle[which, :, :, tile_of(b0)]

    def swap_b_done(which):
        seven = landed.at[which, pl.ds(0, SIDE - 1)]
        remote(seven, seven, swap_send.at[which, 1], swap_recv.at[which, 1], at(a0, around(b0, 1))).wait()

        def body(b, carry):
            for a in range(SIDE):
                row = pl.multiple_of(nat(a, b) * ROWS, ROWS)
                columns[which, pl.ds(row, ROWS), :] = landed[which, b, a]
            return carry

        lax.fori_loop(0, SIDE, body, 0)

    def ring(which, way, item):
        step = item // 2
        half = (item % 2) if way == 0 else 1 - (item % 2)
        sign = 1 if way == 0 else -1
        begin = around(a0, -sign * step) * SIDE + half * (SIDE // 2)
        block = green.at[which, pl.ds(begin, SIDE // 2)]
        return remote(
            block, block, ring_send.at[which, way, item], ring_recv.at[which, way, item], at(around(a0, sign), b0)
        )

    def ring_arrival(which, way, item):
        step = item // 2 + 1
        half = (item % 2) if way == 0 else 1 - (item % 2)
        sign = 1 if way == 0 else -1
        begin = around(a0, -sign * step) * SIDE + half * (SIDE // 2)
        block = green.at[which, pl.ds(begin, SIDE // 2)]
        return remote(
            block, block, ring_send.at[which, way, item], ring_recv.at[which, way, item], at(around(a0, sign), b0)
        )

    def ring_start(which):
        for item in range(2):
            for way in range(2):
                ring(which, way, item).start()

    def ring_step(which, item):
        for way in range(2):
            ring_arrival(which, way, item).wait_recv()
            if item + 2 < ITEMS:
                ring(which, way, item + 2).start()

    def ring_drain(which):
        for item in range(ITEMS):
            for way in range(2):
                ring(which, way, item).wait_send()

    def add_vir(a):
        chunk = green[0, pl.ds(a * SIDE, SIDE)].reshape(CHUNK, ORBS)
        total[...] += jnp.dot(left_side[a], chunk, preferred_element_type=F32)

    def put_occ(a):
        chunk = green[1, pl.ds(a * SIDE, SIDE)].reshape(CHUNK, ORBS)
        part = jnp.dot(chunk, columns[0], preferred_element_type=F32).astype(BF16)
        for b in range(SIDE):
            row = pl.multiple_of(nat(a, b) * ROWS, ROWS)
            occ_out[0, pl.ds(row, ROWS), :] = part[b * ROWS : (b + 1) * ROWS]

    first(0)
    swap_a(0)
    first(1)

    target = lax.broadcasted_iota(jnp.int32, (256, WIDE), 1)
    target = (target % 128) * RB + target // 128

    def fill(i, carry):
        row = lax.broadcasted_iota(jnp.int32, (256, WIDE), 0) + i * 256
        perm[pl.ds(pl.multiple_of(i * 256, 256), 256), :] = jnp.where(row == target, 1.0, 0.0).astype(BF16)
        return carry

    lax.fori_loop(0, WIDE // 256, fill, 0)
    total[...] = jnp.zeros_like(total)
    apart = jnp.dot(
        spread[0].reshape(CHUNK, WIDE), perm[...], preferred_element_type=F32
    ).astype(BF16)
    for a in range(SIDE):
        for q in range(RB):
            left_side[a, q * ROWS : (q + 1) * ROWS, :] = apart[a * ROWS : (a + 1) * ROWS, q * 128 : (q + 1) * 128]

    first_done(0)
    ring_start(0)
    swap_a_done(0)
    swap_b(0)
    add_vir(a0)
    first_done(1)
    for item in range(ITEMS):
        ring_step(0, item)
        if item == 3:
            ring_start(1)
        if item % 2 == 1:
            step = item // 2 + 1
            add_vir(around(a0, -step))
            add_vir(around(a0, step))
        elif item == ITEMS - 1:
            add_vir(around(a0, SIDE // 2))

    for c in range(SIDE):
        for q in range(RB):
            mixed[c * ROWS : (c + 1) * ROWS, q * 128 : (q + 1) * 128] = total[
                q * ROWS : (q + 1) * ROWS, c * 128 : (c + 1) * 128
            ].astype(BF16)
    merged = lax.dot_general(
        mixed[...], perm[...], (((1,), (1,)), ((), ())), preferred_element_type=F32
    ).astype(BF16)
    for c in range(SIDE):
        vir_out[0, :, c * WIDE : (c + 1) * WIDE] = merged[c * ROWS : (c + 1) * ROWS]

    def lay_vir(a, carry):
        for b in range(SIDE):
            spread[1, a, :, b * TILE : (b + 1) * TILE] = vir_out[0, :, tile_of(nat(a, b))]
        return carry

    lax.fori_loop(0, SIDE, lay_vir, 0)
    swap_a(1)

    swap_b_done(0)
    put_occ(a0)
    for item in range(ITEMS):
        ring_step(1, item)
        if item % 2 == 1:
            step = item // 2 + 1
            put_occ(around(a0, -step))
            put_occ(around(a0, step))
        elif item == ITEMS - 1:
            put_occ(around(a0, SIDE // 2))
        if item == 3:
            swap_a_done(1)
            swap_b(1)
    swap_b_done(1)

    gram = lax.dot_general(
        occ_out[0], columns[1], (((0,), (0,)), ((), ())), preferred_element_type=F32
    )
    row = lax.broadcasted_iota(jnp.int32, (TILE, TILE), 0)
    col = lax.broadcasted_iota(jnp.int32, (TILE, TILE), 1)
    gram = jnp.where(row // RB == col // RB, gram, 0.0)
    share = jnp.sum(gram.reshape(ROWS, RB, TILE), axis=0)
    for shift in (8, 16, 32, 64):
        share = share + pltpu.roll(share, shift, 1)

    def exchange(stage, mine, where, value):
        shares[stage, mine] = value

        def body(i, carry):
            block = shares.at[stage, mine]
            remote(block, block, chi_send.at[stage], chi_recv.at[stage], where(i)).start()
            return carry

        lax.fori_loop(1, SIDE, body, 0)
        seven = shares.at[stage, pl.ds(0, SIDE - 1)]
        remote(seven, seven, chi_send.at[stage], chi_recv.at[stage], where(1)).wait()
        return jnp.sum(shares[stage], axis=0)

    share = exchange(0, a0, lambda i: at(around(a0, i), b0), share)
    share = exchange(1, b0, lambda i: at(a0, around(b0, i)), share)
    share = exchange(2, rep_ix, lambda i: (grid_ix, around(rep_ix, i)), share)
    chi_out[...] = share[:, :RB] * scale
    ring_drain(0)
    ring_drain(1)


def per_device(b_tensor, green_occ, green_vir, b_pattern, g_pattern):
    scale = -1.0 / (ORBS * math.sqrt(lax.axis_size("rep")))
    vmem = pl.BlockSpec(memory_space=pltpu.VMEM)
    smem = pl.BlockSpec(memory_space=pltpu.SMEM)
    return pl.pallas_call(
        functools.partial(kernel, scale),
        out_shape=(
            jax.ShapeDtypeStruct((1, ORBS, TILE), BF16),
            jax.ShapeDtypeStruct((1, ROWS, ORBS * RB), BF16),
            jax.ShapeDtypeStruct((RB, RB), F32),
        ),
        in_specs=[vmem, vmem, vmem, smem, smem],
        out_specs=(vmem, vmem, vmem),
        scratch_shapes=[
            pltpu.VMEM((2, SIDE * SIDE, ROWS, ORBS), BF16),
            pltpu.VMEM((2, SIDE, ROWS, WIDE), BF16),
            pltpu.VMEM((2, SIDE, ROWS, WIDE), BF16),
            pltpu.VMEM((2, SIDE, SIDE, ROWS, TILE), BF16),
            pltpu.VMEM((2, ORBS, TILE), BF16),
            pltpu.VMEM((WIDE, WIDE), BF16),
            pltpu.VMEM((SIDE, CHUNK, 128), BF16),
            pltpu.VMEM((CHUNK, ORBS), F32),
            pltpu.VMEM((CHUNK, ORBS), BF16),
            pltpu.VMEM((3, SIDE, RB, TILE), F32),
            pltpu.SemaphoreType.DMA((2,)),
            pltpu.SemaphoreType.DMA((2,)),
            pltpu.SemaphoreType.DMA((2, 2, ITEMS)),
            pltpu.SemaphoreType.DMA((2, 2, ITEMS)),
            pltpu.SemaphoreType.DMA((2, 2)),
            pltpu.SemaphoreType.DMA((2, 2)),
            pltpu.SemaphoreType.DMA((3,)),
            pltpu.SemaphoreType.DMA((3,)),
        ],
        compiler_params=pltpu.CompilerParams(
            collective_id=0, has_side_effects=True, vmem_limit_bytes=40 * 1024 * 1024
        ),
        cost_estimate=pl.CostEstimate(flops=600_000_000, bytes_accessed=1_200_000, transcendentals=0),
    )(b_tensor, green_occ, green_vir, b_pattern, g_pattern)


def solution(mesh):
    return jax.shard_map(
        per_device,
        mesh=mesh,
        in_specs=(
            P("rep", "grid", None),
            P("rep", "grid", None),
            P("rep", "grid", None),
            P("rep", None, None),
            P("rep", None, None),
        ),
        out_specs=(P("rep", None, "grid"), P("rep", "grid", None), P()),
        check_vma=False,
    )
```

```python
import functools
import math

import jax
import jax.numpy as jnp
from jax import lax
from jax.experimental import pallas as pl
from jax.experimental.pallas import tpu as pltpu
from jax.sharding import PartitionSpec as P

MESH = pl.DeviceIdType.MESH
SIDE = 8
PLANE = SIDE * SIDE
HALF = SIDE // 2
ROWS = 16
ORBS = 1024
RB = 8
TILE = ROWS * RB
WIDE = SIDE * TILE
F32 = jnp.float32
BF16 = jnp.bfloat16


def around(index, step):
    return lax.rem(index + (step + SIDE), SIDE)


def kernel(
    scale,
    b_hbm,
    occ_hbm,
    vir_hbm,
    bp_hbm,
    gp_hbm,
    occ_out,
    vir_out,
    chi_out,
    b_ref,
    occ_ref,
    vir_ref,
    bp_ref,
    gp_ref,
    vir_own,
    vir_all,
    occ_all,
    spread,
    other,
    middle,
    landed,
    landed_two,
    both,
    perm,
    sort,
    left_side,
    total,
    mixed,
    merged,
    vir_land,
    vir_back,
    occ_own,
    occ_two,
    occ_back,
    shares,
    shares_rep,
    io_sem,
    vir_one_send,
    vir_one_recv,
    occ_one_send,
    occ_one_recv,
    vir_ring_send,
    vir_ring_recv,
    occ_ring_send,
    occ_ring_recv,
    swap_send,
    swap_recv,
    pair_send,
    pair_recv,
    chi_send,
    chi_recv,
):
    grid_ix = lax.axis_index("grid")
    rep_ix = lax.axis_index("rep")
    z, y = grid_ix // SIDE, grid_ix % SIDE
    core = rep_ix % 2
    a0 = z + core * (y - z)
    b0 = y + core * (z - y)
    sa = SIDE - (SIDE - 1) * core
    sb = 1 + (SIDE - 1) * core
    par = b0 % 2
    jb = b0 // 2
    vir_mate = around(b0, 2 * par - 1)
    occ_mate = around(b0, 1 - 2 * par)

    def nat(a, b):
        return a * sa + b * sb

    def at(a, b):
        return (nat(a, b), rep_ix)

    def remote(src, dst, send, recv, where):
        return pltpu.make_async_remote_copy(
            src_ref=src, dst_ref=dst, send_sem=send, recv_sem=recv, device_id=where, device_id_type=MESH
        )

    def tile_of(i):
        return pl.ds(pl.multiple_of(i * TILE, TILE), TILE)

    def rows_of(i):
        return pl.ds(pl.multiple_of(i * ROWS, ROWS), ROWS)

    barrier = pltpu.get_barrier_semaphore()

    def greet(i, carry):
        for where in (at(around(a0, i), b0), at(a0, around(b0, i)), (grid_ix, around(rep_ix, i))):
            pl.semaphore_signal(barrier, inc=1, device_id=where, device_id_type=MESH)
        return carry

    lax.fori_loop(1, SIDE, greet, 0)

    loads = [
        pltpu.make_async_copy(src, dst, io_sem.at[i])
        for i, (src, dst) in enumerate(
            ((gp_hbm, gp_ref), (vir_hbm, vir_ref), (bp_hbm, bp_ref), (b_hbm, b_ref), (occ_hbm, occ_ref))
        )
    ]
    for load in loads:
        load.start()

    def fill_sort(i, carry):
        m = lax.broadcasted_iota(jnp.int32, (256, ORBS), 1)
        a, b = (m // ROWS) % SIDE, 2 * ((m // 128) % HALF) + m // 512
        source = (a * sa + b * sb) * ROWS + m % ROWS
        row = lax.broadcasted_iota(jnp.int32, (256, ORBS), 0) + i * 256
        sort[pl.ds(pl.multiple_of(i * 256, 256), 256), :] = jnp.where(row == source, 1.0, 0.0).astype(BF16)
        return carry

    lax.fori_loop(0, ORBS // 256, fill_sort, 0)

    molecule = grid_ix // 4
    lane = lax.broadcasted_iota(jnp.int32, (ROWS, 128), 1)
    loads[0].wait()
    loads[1].wait()
    keeps = [
        jnp.where(lane < 64, gp_ref[0, molecule, 2 * t], gp_ref[0, molecule, 2 * t + 1]).astype(F32).astype(BF16)
        for t in range(SIDE)
    ]
    for t in range(SIDE):
        cols = slice(t * 128, (t + 1) * 128)
        vir_ref[0, :, cols] = vir_ref[0, :, cols] * keeps[t]
    sorted_vir = jnp.dot(vir_ref[0], sort[...], preferred_element_type=F32).astype(BF16)
    vir_own[0] = sorted_vir[:, :512]
    vir_own[1] = sorted_vir[:, 512:]
    vir_all[a0 * SIDE + b0] = vir_own[par]

    loads[2].wait()
    loads[3].wait()

    def lay(a, carry):
        for b in range(SIDE):
            n = nat(a, b)
            keep = jnp.full((ROWS, TILE), bp_ref[0, molecule, n // 4], jnp.int32).astype(F32).astype(BF16)
            spread[a, :, b * TILE : (b + 1) * TILE] = b_ref[0, :, tile_of(n)] * keep
        return carry

    lax.fori_loop(0, SIDE, lay, 0)
    loads[4].wait()
    for t in range(SIDE):
        cols = slice(t * 128, (t + 1) * 128)
        occ_all[a0 * HALF + jb, :, cols] = occ_ref[0, :, cols] * keeps[t]

    pl.semaphore_wait(barrier, 3 * (SIDE - 1))

    def near(k):
        return ((k + 1) // 2) * (2 * (k % 2) - 1)

    def vir_block(a, k):
        return vir_all.at[a * SIDE + around(b0, near(k))]

    def occ_block(a, k):
        return occ_all.at[a * HALF + around(b0, 2 * near(k)) // 2]

    def vir_one(b):
        return remote(
            vir_own.at[b % 2], vir_all.at[a0 * SIDE + b0], vir_one_send.at[b], vir_one_recv.at[b0], at(a0, b)
        )

    def vir_one_arrival(b):
        block = vir_all.at[a0 * SIDE + b]
        return remote(block, block, vir_one_send.at[b], vir_one_recv.at[b], at(a0, b))

    def occ_one(b):
        block = occ_all.at[a0 * HALF + jb]
        return remote(block, block, occ_one_send.at[b // 2], occ_one_recv.at[jb], at(a0, b))

    def occ_one_arrival(b):
        block = occ_all.at[a0 * HALF + b // 2]
        return remote(block, block, occ_one_send.at[b // 2], occ_one_recv.at[b // 2], at(a0, b))

    def hop(block, send, recv, way, d, k):
        sign = 1 - 2 * way
        piece = block(around(a0, -sign * (d - 1)), k)
        return remote(piece, piece, send.at[way, d - 1, k], recv.at[way, d - 1, k], at(around(a0, sign), b0))

    def arrival(block, send, recv, way, d, k):
        sign = 1 - 2 * way
        piece = block(around(a0, -sign * d), k)
        return remote(piece, piece, send.at[way, d - 1, k], recv.at[way, d - 1, k], at(around(a0, sign), b0))

    vir_ring = (vir_block, vir_ring_send, vir_ring_recv)
    occ_ring = (occ_block, occ_ring_send, occ_ring_recv)

    def ring_begin(ring, count, one_arrival, stride):
        def body(k, carry):
            one_arrival(around(b0, stride * near(k))).wait_recv()
            hop(*ring, 0, 1, k).start()
            hop(*ring, 1, 1, k).start()
            return carry

        hop(*ring, 0, 1, 0).start()
        hop(*ring, 1, 1, 0).start()
        lax.fori_loop(1, count, body, 0)

    def ring_step(ring, count, d):
        def body(low, high, k, carry):
            if d < 4 or low:
                arrival(*ring, 0, d, k).wait_recv()
                if d < 3 or (d == 3 and low):
                    hop(*ring, 0, d + 1, k).start()
            if d < 4 or high:
                arrival(*ring, 1, d, k).wait_recv()
                if d < 3 or (d == 3 and high):
                    hop(*ring, 1, d + 1, k).start()
            return carry

        lax.fori_loop(0, count // 2, functools.partial(body, True, False), 0)
        lax.fori_loop(count // 2, count, functools.partial(body, False, True), 0)

    def ring_drain(ring, count):
        def body(low, k, carry):
            for d in range(1, 4):
                hop(*ring, 0, d, k).wait_send()
                hop(*ring, 1, d, k).wait_send()
            hop(*ring, 0 if low else 1, 4, k).wait_send()
            return carry

        lax.fori_loop(0, count // 2, functools.partial(body, True), 0)
        lax.fori_loop(count // 2, count, functools.partial(body, False), 0)

    def vir_one_start(i, carry):
        vir_one(around(b0, i)).start()
        return carry

    lax.fori_loop(1, SIDE, vir_one_start, 0)

    def swap_a(i, carry):
        a = around(a0, i)
        remote(spread.at[a], middle.at[a0], swap_send.at[0], swap_recv.at[0], at(a, b0)).start()
        return carry

    def swap_b(i, carry):
        b = around(b0, i)
        remote(
            middle.at[:, :, tile_of(b)], landed.at[b0], swap_send.at[1], swap_recv.at[1], at(a0, b)
        ).start()
        return carry

    pair_spread = remote(spread, other, pair_send.at[0], pair_recv.at[0], at(a0, vir_mate))
    pair_landed = remote(landed, landed_two, pair_send.at[1], pair_recv.at[1], at(a0, occ_mate))
    pair_vir = remote(
        merged.at[pl.ds(PLANE, PLANE)], vir_back, pair_send.at[2], pair_recv.at[2], at(a0, vir_mate)
    )
    pair_occ = remote(occ_two, occ_back, pair_send.at[3], pair_recv.at[3], at(a0, occ_mate))

    lax.fori_loop(1, SIDE, swap_a, 0)
    middle[a0] = spread[a0]
    pair_spread.start()
    for step in (2, 6, 4):
        occ_one(around(b0, step)).start()

    target = lax.broadcasted_iota(jnp.int32, (256, WIDE), 1)
    target = (target % 128) * RB + target // 128

    def fill(i, carry):
        row = lax.broadcasted_iota(jnp.int32, (256, WIDE), 0) + i * 256
        perm[pl.ds(pl.multiple_of(i * 256, 256), 256), :] = jnp.where(row == target, 1.0, 0.0).astype(BF16)
        return carry

    def part(w, source):
        apart = jnp.dot(source[...].reshape(128, WIDE), perm[...], preferred_element_type=F32).astype(BF16)
        for a in range(SIDE):
            for q in range(RB):
                row = w * 128 + q * ROWS
                left_side[a, row : row + ROWS, :] = apart[a * ROWS : (a + 1) * ROWS, q * 128 : (q + 1) * 128]

    def add_vir(a):
        chunk = vir_all[pl.ds(a * SIDE, SIDE)].reshape(128, 512)
        total[...] += jnp.dot(left_side[a], chunk, preferred_element_type=F32)

    def put_occ(a):
        chunk = occ_all[pl.ds(a * HALF, HALF)].reshape(64, ORBS)
        product = jnp.dot(chunk, both[...], preferred_element_type=F32).astype(BF16)
        rows = pl.ds(pl.multiple_of(a * 64, 64), 64)
        occ_own[rows, :] = product[:, :TILE]
        occ_two[rows, :] = product[:, TILE:]

    ring_begin(vir_ring, SIDE, vir_one_arrival, 1)
    lax.fori_loop(0, WIDE // 256, fill, 0)
    total[...] = jnp.zeros_like(total)
    part(0, spread)
    ring_begin(occ_ring, HALF, occ_one_arrival, 2)

    ring_step(vir_ring, SIDE, 1)

    seven = middle.at[pl.ds(0, SIDE - 1)]
    remote(seven, seven, swap_send.at[0], swap_recv.at[0], at(around(a0, 1), b0)).wait()
    lax.fori_loop(1, SIDE, swap_b, 0)
    landed[b0] = middle[:, :, tile_of(b0)]
    pair_spread.wait()
    part(1, other)
    add_vir(a0)

    ring_step(occ_ring, HALF, 1)
    ring_step(vir_ring, SIDE, 2)
    add_vir(around(a0, -1))
    add_vir(around(a0, 1))
    ring_step(occ_ring, HALF, 2)
    ring_step(vir_ring, SIDE, 3)
    add_vir(around(a0, -2))
    add_vir(around(a0, 2))

    seven = landed.at[pl.ds(0, SIDE - 1)]
    remote(seven, seven, swap_send.at[1], swap_recv.at[1], at(a0, around(b0, 1))).wait()
    pair_landed.start()

    ring_step(occ_ring, HALF, 3)
    add_vir(around(a0, -3))
    add_vir(around(a0, 3))
    ring_step(vir_ring, SIDE, 4)
    add_vir(around(a0, 4))

    for w in range(2):
        for j in range(HALF):
            for q in range(RB):
                row, new = (w * RB + q) * ROWS, (w * HALF + j) * ROWS
                mixed[new : new + ROWS, q * 128 : (q + 1) * 128] = total[
                    row : row + ROWS, j * 128 : (j + 1) * 128
                ].astype(BF16)
    merged[...] = lax.dot_general(
        mixed[...], perm[...], (((1,), (1,)), ((), ())), preferred_element_type=F32
    ).astype(BF16)

    def vir_own_swap(i, carry):
        a, j = around(a0, i // HALF), (jb + i) % HALF
        remote(
            merged.at[rows_of(j), tile_of(a)],
            vir_land.at[a0 * HALF + jb],
            swap_send.at[2],
            swap_recv.at[2],
            at(a, 2 * j + par),
        ).start()
        return carry

    def vir_mate_swap(i, carry):
        a, j = around(a0, i // HALF), (jb + i) % HALF
        remote(
            merged.at[rows_of(HALF + j), tile_of(a)],
            vir_land.at[PLANE // 2 + a0 * HALF + vir_mate // 2],
            swap_send.at[2],
            swap_recv.at[2],
            at(a, around(2 * j + par, 1 - 2 * par)),
        ).start()
        return carry

    lax.fori_loop(1, PLANE // 2, vir_own_swap, 0)
    lax.fori_loop(0, PLANE // 2, vir_mate_swap, 0)
    vir_land[a0 * HALF + jb] = merged[rows_of(jb), tile_of(a0)]
    pair_vir.start()

    pair_landed.wait()

    def join(b, carry):
        for a in range(SIDE):
            rows = rows_of(nat(a, b))
            both[rows, :TILE] = landed[b, a]
            both[rows, TILE:] = landed_two[b, a]
        return carry

    lax.fori_loop(0, SIDE, join, 0)
    put_occ(a0)
    for d in range(1, 4):
        put_occ(around(a0, -d))
        put_occ(around(a0, d))
    ring_step(occ_ring, HALF, 4)
    put_occ(around(a0, 4))
    pair_occ.start()

    most = vir_land.at[pl.ds(0, PLANE - 1)]
    remote(most, most, swap_send.at[2], swap_recv.at[2], at(a0, around(b0, 1))).wait()

    gram = jnp.zeros((TILE, TILE), F32)
    for c, mine in enumerate((occ_own, occ_two)):
        theirs = vir_land[c * PLANE // 2 : (c + 1) * PLANE // 2].reshape(512, TILE)
        gram += lax.dot_general(mine[...], theirs, (((0,), (0,)), ((), ())), preferred_element_type=F32)
    row = lax.broadcasted_iota(jnp.int32, (TILE, TILE), 0)
    col = lax.broadcasted_iota(jnp.int32, (TILE, TILE), 1)
    gram = jnp.where(row // RB == col // RB, gram, 0.0)
    share = jnp.sum(gram.reshape(ROWS, RB, TILE), axis=0)

    def fold(values):
        for shift in (8, 16, 32, 64):
            values = values + pltpu.roll(values, shift, 1)
        return values

    place = lax.broadcasted_iota(jnp.int32, (RB, TILE), 1) // RB == lax.broadcasted_iota(jnp.int32, (RB, TILE), 0)
    share = jnp.sum(jnp.where(place, fold(share), 0.0), axis=0, keepdims=True)

    shares[pl.ds(grid_ix, 1), :] = share

    def tell(i, carry):
        line = shares.at[pl.ds(grid_ix, 1)]
        remote(line, line, chi_send.at[0], chi_recv.at[0], (lax.rem(grid_ix + i, PLANE), rep_ix)).start()
        return carry

    lax.fori_loop(1, PLANE, tell, 0)
    for a in range(SIDE):
        for j in range(HALF):
            vir_out[0, :, tile_of(nat(a, 2 * j + par))] = merged[j * ROWS : (j + 1) * ROWS, a * TILE : (a + 1) * TILE]
            occ_out[0, rows_of(nat(a, 2 * j + par)), :] = occ_own[(a * HALF + j) * ROWS : (a * HALF + j + 1) * ROWS]
    pair_vir.wait()
    for a in range(SIDE):
        for j in range(HALF):
            vir_out[0, :, tile_of(nat(a, 2 * j + 1 - par))] = vir_back[
                j * ROWS : (j + 1) * ROWS, a * TILE : (a + 1) * TILE
            ]
    pair_occ.wait()
    for a in range(SIDE):
        for j in range(HALF):
            occ_out[0, rows_of(nat(a, 2 * j + 1 - par)), :] = occ_back[
                (a * HALF + j) * ROWS : (a * HALF + j + 1) * ROWS
            ]
    ring_drain(vir_ring, SIDE)
    ring_drain(occ_ring, HALF)

    def vir_one_drain(i, carry):
        vir_one(around(b0, i)).wait_send()
        return carry

    lax.fori_loop(1, SIDE, vir_one_drain, 0)
    for step in (2, 6, 4):
        occ_one(around(b0, step)).wait_send()

    lines = shares.at[pl.ds(0, PLANE - 1)]
    remote(lines, lines, chi_send.at[0], chi_recv.at[0], at(a0, around(b0, 1))).wait()
    shares_rep[pl.ds(rep_ix, 1), :] = jnp.sum(shares[...], axis=0, keepdims=True)

    def tell_rep(i, carry):
        line = shares_rep.at[pl.ds(rep_ix, 1)]
        remote(line, line, chi_send.at[1], chi_recv.at[1], (grid_ix, around(rep_ix, i))).start()
        return carry

    lax.fori_loop(1, SIDE, tell_rep, 0)
    lines = shares_rep.at[pl.ds(0, SIDE - 1)]
    remote(lines, lines, chi_send.at[1], chi_recv.at[1], (grid_ix, around(rep_ix, 1))).wait()
    share = jnp.sum(shares_rep[...], axis=0, keepdims=True) * scale
    share = fold(jnp.where(place, jnp.broadcast_to(share, (RB, TILE)), 0.0))
    chi_out[...] = share[:, :RB]


def per_device(b_tensor, green_occ, green_vir, b_pattern, g_pattern):
    scale = -1.0 / (ORBS * math.sqrt(lax.axis_size("rep")))
    vmem = pl.BlockSpec(memory_space=pltpu.VMEM)
    hbm = pl.BlockSpec(memory_space=pltpu.HBM)
    dma = pltpu.SemaphoreType.DMA
    return pl.pallas_call(
        functools.partial(kernel, scale),
        out_shape=(
            jax.ShapeDtypeStruct((1, ORBS, TILE), BF16),
            jax.ShapeDtypeStruct((1, ROWS, ORBS * RB), BF16),
            jax.ShapeDtypeStruct((RB, RB), F32),
        ),
        in_specs=[hbm] * 5,
        out_specs=(vmem, vmem, vmem),
        scratch_shapes=[
            pltpu.VMEM(b_tensor.shape, BF16),
            pltpu.VMEM(green_occ.shape, BF16),
            pltpu.VMEM(green_vir.shape, BF16),
            pltpu.SMEM(b_pattern.shape, jnp.int32),
            pltpu.SMEM(g_pattern.shape, jnp.int32),
            pltpu.VMEM((2, ROWS, 512), BF16),
            pltpu.VMEM((PLANE, ROWS, 512), BF16),
            pltpu.VMEM((PLANE // 2, ROWS, ORBS), BF16),
            pltpu.VMEM((SIDE, ROWS, WIDE), BF16),
            pltpu.VMEM((SIDE, ROWS, WIDE), BF16),
            pltpu.VMEM((SIDE, ROWS, WIDE), BF16),
            pltpu.VMEM((SIDE, SIDE, ROWS, TILE), BF16),
            pltpu.VMEM((SIDE, SIDE, ROWS, TILE), BF16),
            pltpu.VMEM((ORBS, 2 * TILE), BF16),
            pltpu.VMEM((WIDE, WIDE), BF16),
            pltpu.VMEM((ORBS, ORBS), BF16),
            pltpu.VMEM((SIDE, 256, 128), BF16),
            pltpu.VMEM((256, 512), F32),
            pltpu.VMEM((128, WIDE), BF16),
            pltpu.VMEM((128, WIDE), BF16),
            pltpu.VMEM((PLANE, ROWS, TILE), BF16),
            pltpu.VMEM((PLANE, WIDE), BF16),
            pltpu.VMEM((512, TILE), BF16),
            pltpu.VMEM((512, TILE), BF16),
            pltpu.VMEM((512, TILE), BF16),
            pltpu.VMEM((PLANE, TILE), F32),
            pltpu.VMEM((SIDE, TILE), F32),
            dma((5,)),
            dma((SIDE,)),
            dma((SIDE,)),
            dma((HALF,)),
            dma((HALF,)),
            dma((2, 4, SIDE)),
            dma((2, 4, SIDE)),
            dma((2, 4, HALF)),
            dma((2, 4, HALF)),
            dma((3,)),
            dma((3,)),
            dma((4,)),
            dma((4,)),
            dma((2,)),
            dma((2,)),
        ],
        compiler_params=pltpu.CompilerParams(
            collective_id=0, has_side_effects=True, vmem_limit_bytes=56 * 1024 * 1024
        ),
        cost_estimate=pl.CostEstimate(flops=600_000_000, bytes_accessed=1_200_000, transcendentals=0),
    )(b_tensor, green_occ, green_vir, b_pattern, g_pattern)


def solution(mesh):
    return jax.shard_map(
        per_device,
        mesh=mesh,
        in_specs=(
            P("rep", "grid", None),
            P("rep", "grid", None),
            P("rep", "grid", None),
            P("rep", None, None),
            P("rep", None, None),
        ),
        out_specs=(P("rep", None, "grid"), P("rep", "grid", None), P()),
        check_vma=False,
    )
```

```python
import functools
import math

import jax
import jax.numpy as jnp
from jax import lax
from jax.experimental import pallas as pl
from jax.experimental.pallas import tpu as pltpu
from jax.sharding import PartitionSpec as P

MESH = pl.DeviceIdType.MESH
SIDE = 8
PLANE = SIDE * SIDE
HALF = SIDE // 2
ROWS = 16
ORBS = 1024
RB = 8
TILE = ROWS * RB
WIDE = SIDE * TILE
F32 = jnp.float32
BF16 = jnp.bfloat16


def around(index, step):
    return lax.rem(index + (step + SIDE), SIDE)


FAR = [4, 5, 3, 6, 2, 7, 1]
SUBS = 4


def kernel(
    scale,
    b_hbm,
    occ_hbm,
    vir_hbm,
    bp_hbm,
    gp_hbm,
    occ_out,
    vir_out,
    chi_out,
    b_ref,
    occ_ref,
    vir_ref,
    bp_ref,
    gp_ref,
    vir_own,
    vir_all,
    occ_all,
    strips,
    left_side,
    landed,
    both,
    perm,
    mixed,
    merged,
    vir_land,
    vir_back,
    occ_pair,
    occ_two,
    occ_back,
    shares,
    shares_rep,
    io_sem,
    vir_send,
    vir_recv,
    occ_one_send,
    occ_one_recv,
    occ_ring_send,
    occ_ring_recv,
    strip_send,
    strip_recv,
    swap_send,
    swap_recv,
    chi_send,
    chi_recv,
):
    grid_ix = lax.axis_index("grid")
    rep_ix = lax.axis_index("rep")
    z, y = grid_ix // SIDE, grid_ix % SIDE
    core = rep_ix % 2
    a0 = z + core * (y - z)
    b0 = y + core * (z - y)
    sa = SIDE - (SIDE - 1) * core
    sb = 1 + (SIDE - 1) * core
    par = b0 % 2
    jb = b0 // 2
    mate = around(b0, 1 - 2 * par)
    abs_a = [around(a0, i) for i in range(SIDE)]
    abs_b = [around(b0, j) for j in range(SIDE)]
    part_a = [a * sa for a in abs_a]
    part_b = [b * sb for b in abs_b]

    def nat(i, j):
        return part_a[i % SIDE] + part_b[j % SIDE]

    def at(i, j):
        return (nat(i, j), rep_ix)

    def at_mate(i):
        return (part_a[i % SIDE] + mate * sb, rep_ix)

    def remote(src, dst, send, recv, where):
        return pltpu.make_async_remote_copy(
            src_ref=src, dst_ref=dst, send_sem=send, recv_sem=recv, device_id=where, device_id_type=MESH
        )

    def send(*copy):
        remote(*copy).start()

    def tile_of(i):
        return pl.ds(pl.multiple_of(i * TILE, TILE), TILE)

    def rows_of(i, count=ROWS):
        return pl.ds(pl.multiple_of(i * count, count), count)

    barrier = pltpu.get_barrier_semaphore()
    for i in range(1, SIDE):
        for where in (at(i, 0), at(0, i), (grid_ix, around(rep_ix, i))):
            pl.semaphore_signal(barrier, inc=1, device_id=where, device_id_type=MESH)

    loads = [
        pltpu.make_async_copy(src, dst, io_sem.at[i])
        for i, (src, dst) in enumerate(
            ((gp_hbm, gp_ref), (vir_hbm, vir_ref), (bp_hbm, bp_ref), (b_hbm, b_ref), (occ_hbm, occ_ref))
        )
    ]
    for load in loads:
        load.start()

    molecule = grid_ix // 4
    lane = lax.broadcasted_iota(jnp.int32, (ROWS, 128), 1)
    loads[0].wait()
    loads[1].wait()
    keeps = [
        jnp.where(lane < 64, gp_ref[0, molecule, 2 * t], gp_ref[0, molecule, 2 * t + 1]).astype(F32)
        for t in range(SIDE)
    ]
    tiles = [vir_ref[0, :, t * 128 : (t + 1) * 128].astype(F32) * keeps[t] for t in range(SIDE)]
    for bit in (1, 2, 4):
        high = (lane // ROWS // bit) % 2 + 2 * core
        for t in range(SIDE):
            if t & bit == 0:
                u = t + bit
                low_tile = jnp.where(high == 1, pltpu.roll(tiles[u], ROWS * bit, 1), tiles[t])
                high_tile = jnp.where(high == 0, pltpu.roll(tiles[t], 128 - ROWS * bit, 1), tiles[u])
                tiles[t], tiles[u] = low_tile, high_tile
    for b in range(SIDE):
        vir_own[b] = tiles[b].astype(BF16)
    vir_all[0, b0] = vir_own[b0]

    loads[2].wait()
    loads[3].wait()
    for m in range(2 * SIDE):
        keep = jnp.full((ROWS, 512), bp_ref[0, molecule, m], jnp.int32).astype(F32).astype(BF16)
        cols = slice(m * 512, (m + 1) * 512)
        b_ref[0, :, cols] = b_ref[0, :, cols] * keep
    for i in range(SIDE):
        for b in range(SIDE):
            strips[0, i, :, b * TILE : (b + 1) * TILE] = b_ref[0, :, tile_of(part_a[i] + b * sb)]
    loads[4].wait()
    for t in range(SIDE):
        cols = slice(t * 128, (t + 1) * 128)
        occ_all[0, 0, :, cols] = occ_ref[0, :, cols] * keeps[t].astype(BF16)

    pl.semaphore_wait(barrier, 3 * (SIDE - 1))

    for j in FAR:
        send(vir_own.at[abs_b[j]], vir_all.at[0, b0], vir_send.at[0], vir_recv.at[0], at(0, j))

    def strip_ring(way, d, u):
        sign = 1 - 2 * way
        send(
            strips.at[-sign * (d - 1) % SIDE, pl.ds(2 * u, 2)],
            strips.at[-sign * d % SIDE, pl.ds(2 * u, 2)],
            strip_send,
            strip_recv.at[way, SUBS * (d - 1) + u % (SUBS if d < 4 else SUBS // 2)],
            at(0, sign),
        )

    def strip_wait(way, d, u):
        piece = strips.at[(2 * way - 1) * d % SIDE, pl.ds(2 * u, 2)]
        slot = strip_recv.at[way, SUBS * (d - 1) + u % (SUBS if d < 4 else SUBS // 2)]
        remote(piece, piece, strip_send, slot, at(0, 1)).wait_recv()

    def occ_ring(way, d, g):
        sign = 1 - 2 * way
        send(
            occ_all.at[-sign * (d - 1) % SIDE, pl.ds(2 * g, 2)],
            occ_all.at[-sign * d % SIDE, pl.ds(2 * g, 2)],
            occ_ring_send,
            occ_ring_recv.at[way, 2 * (d - 1) + g if d < 4 else 6],
            at(sign, 0),
        )

    def occ_step(d):
        for g in range(2):
            for way in range(2):
                if d == 4 and g != way:
                    continue
                piece = occ_all.at[(2 * way - 1) * d % SIDE, pl.ds(2 * g, 2)]
                slot = occ_ring_recv.at[way, 2 * (d - 1) + g if d < 4 else 6]
                remote(piece, piece, occ_ring_send, slot, at(1, 0)).wait_recv()
                if d < 3 or (d == 3 and g == way):
                    occ_ring(way, d + 1, g)

    def swap(j):
        pair = pl.ds(pl.multiple_of(jb * 2 * TILE, 2 * TILE), 2 * TILE)
        for i in FAR:
            send(strips.at[j, i, :, pair], landed.at[-i % SIDE, j], swap_send.at[0], swap_recv.at[0], at(i, 0))
        landed[0, j] = strips[j, 0, :, pair]

    def fill(i, carry):
        target = lax.broadcasted_iota(jnp.int32, (256, WIDE), 1)
        target = (target % 128) * RB + target // 128
        row = lax.broadcasted_iota(jnp.int32, (256, WIDE), 0) + i * 256
        perm[pl.ds(pl.multiple_of(i * 256, 256), 256), :] = jnp.where(row == target, 1.0, 0.0).astype(BF16)
        return carry

    def part(j):
        apart = jnp.dot(strips[j].reshape(128, WIDE), perm[...], preferred_element_type=F32).astype(BF16)
        for i in range(SIDE):
            for q in range(RB):
                left_side[j, q * ROWS : (q + 1) * ROWS, i * 128 : (i + 1) * 128] = apart[
                    i * ROWS : (i + 1) * ROWS, q * 128 : (q + 1) * 128
                ]

    place = [((par + j) % 2) * HALF + abs_b[j] // 2 for j in range(SIDE)]

    def contract(j):
        product = jnp.dot(left_side[j], vir_all[...].reshape(ORBS, 128), preferred_element_type=F32).astype(BF16)
        for q in range(RB):
            mixed[rows_of(place[j]), q * 128 : (q + 1) * 128] = product[q * ROWS : (q + 1) * ROWS]

    for m in (2, 1, 3):
        send(occ_all.at[0, 0], occ_all.at[0, -m % HALF], occ_one_send, occ_one_recv.at[-m % HALF // 2], at(0, 2 * m))
    for u in range(SUBS):
        for way in range(2):
            strip_ring(way, 1, u)
    swap(0)
    lax.fori_loop(0, WIDE // 256, fill, 0)

    blocks = vir_all.at[0, pl.ds(0, SIDE - 1)]
    remote(blocks, blocks, vir_send.at[0], vir_recv.at[0], at(0, 1)).wait()
    for i in FAR:
        send(vir_all.at[0], vir_all.at[-i % SIDE], vir_send.at[1], vir_recv.at[1], at(i, 0))

    def occ_begin():
        for g in range(2):
            blocks = occ_all.at[0, pl.ds(2, 2)] if g else occ_all.at[0, pl.ds(1, 1)]
            remote(blocks, blocks, occ_one_send, occ_one_recv.at[g], at(0, 1)).wait_recv()
            for way in range(2):
                occ_ring(way, 1, g)

    def vir_end():
        chunks = vir_all.at[pl.ds(0, SIDE - 1)]
        remote(chunks, chunks, vir_send.at[1], vir_recv.at[1], at(1, 0)).wait()

    def run(*steps):
        return [functools.partial(*step) for step in steps]

    work = {
        (1, 0): run((part, 0)),
        (1, 2): run((occ_begin,)),
        (2, 0): run((swap, 1), (swap, 7)),
        (2, 1): run((part, 1)),
        (2, 2): run((part, 7)),
        (2, 3): run((occ_step, 1)),
        (3, 0): run((swap, 2), (swap, 6), (vir_end,), (contract, 0)),
        (3, 1): run((part, 2), (contract, 1)),
        (3, 2): run((part, 6), (contract, 7)),
        (3, 3): run((occ_step, 2), (contract, 2), (contract, 6)),
        (4, 0): run((swap, 3), (swap, 5), (part, 3), (contract, 3)),
        (4, 1): run((part, 5), (contract, 5)),
    }
    for d in range(1, 5):
        for u in range(SUBS if d < 4 else SUBS // 2):
            for way in range(2):
                sub = u if d < 4 else u + way * SUBS // 2
                strip_wait(way, d, sub)
                if d < 3 or (d == 3 and u // (SUBS // 2) == way):
                    strip_ring(way, d + 1, sub)
            for step in work.get((d, u), ()):
                step()
    swap(4)
    part(4)
    contract(4)

    merged[...] = lax.dot_general(
        mixed[...], perm[...], (((1,), (1,)), ((), ())), preferred_element_type=F32
    ).astype(BF16)

    for i in FAR + [0]:
        for own in (False, True):
            if not (own and i == 0):
                parity = par if own else 1 - par
                send(
                    merged.at[rows_of(parity, 64), tile_of(abs_a[i])],
                    vir_land.at[par * SIDE + -i % SIDE],
                    swap_send.at[1],
                    swap_recv.at[1],
                    at(i, 0) if own else at_mate(i),
                )
    vir_land[par * SIDE] = merged[rows_of(par, 64), tile_of(a0)]

    for j in FAR:
        send(merged.at[rows_of(place[j])], vir_back.at[-j % SIDE], swap_send.at[2], swap_recv.at[2], at(0, j))
    occ_step(3)
    pieces = landed.at[pl.ds(0, SIDE - 1)]
    remote(pieces, pieces, swap_send.at[0], swap_recv.at[0], at(1, 0)).wait()
    for i in range(SIDE):
        for j in range(SIDE):
            both[rows_of(nat(i, j)), :] = landed[i, j]

    turn = [lax.rem(jb + m, HALF) for m in range(HALF)]

    def put_occ(i):
        product = jnp.dot(occ_all[i].reshape(64, ORBS), both[...], preferred_element_type=F32).astype(BF16)
        for m in range(HALF):
            occ_pair[rows_of(i * HALF + turn[m]), :] = product[m * ROWS : (m + 1) * ROWS]

    for i in (0, 1, 7, 2, 6, 3, 5):
        put_occ(i)
    occ_step(4)
    put_occ(4)
    occ_two[...] = occ_pair[:, tile_of(1 - par)]

    most = vir_land.at[pl.ds(0, 2 * SIDE - 1)]
    remote(most, most, swap_send.at[1], swap_recv.at[1], at(1, 0)).wait()

    gram = jnp.zeros((TILE, TILE), F32)
    for c in range(2):
        mine = occ_pair[:, c * TILE : (c + 1) * TILE]
        theirs = vir_land[c * SIDE : (c + 1) * SIDE].reshape(512, TILE)
        gram += lax.dot_general(mine, theirs, (((0,), (0,)), ((), ())), preferred_element_type=F32)
    row = lax.broadcasted_iota(jnp.int32, (TILE, TILE), 0)
    col = lax.broadcasted_iota(jnp.int32, (TILE, TILE), 1)
    gram = jnp.where(row // RB == col // RB, gram, 0.0)
    share = jnp.sum(gram.reshape(ROWS, RB, TILE), axis=0)

    def fold(values):
        for shift in (8, 16, 32, 64):
            values = values + pltpu.roll(values, shift, 1)
        return values

    spot = lax.broadcasted_iota(jnp.int32, (RB, TILE), 1) // RB == lax.broadcasted_iota(jnp.int32, (RB, TILE), 0)
    share = jnp.sum(jnp.where(spot, fold(share), 0.0), axis=0, keepdims=True)
    shares[pl.ds(grid_ix, 1), :] = share
    line = shares.at[pl.ds(grid_ix, 1)]
    for i in FAR + [0]:
        for j in FAR + [0]:
            if (i, j) != (0, 0):
                send(line, line, chi_send.at[0], chi_recv.at[0], at(i, j))

    pair_occ = remote(occ_two, occ_back, swap_send.at[3], swap_recv.at[3], at_mate(0))
    pair_occ.start()
    for a in range(SIDE):
        vir_out[0, :, tile_of(a * sa + part_b[0])] = merged[rows_of(place[0]), a * TILE : (a + 1) * TILE]
    for i in range(SIDE):
        for m in range(HALF):
            rows = rows_of(part_a[i] + (2 * m + par) * sb)
            occ_out[0, rows, :] = occ_pair[(i * HALF + m) * ROWS : (i * HALF + m + 1) * ROWS, tile_of(par)]
    for piece, sem in (
        (occ_all.at[0, pl.ds(0, HALF - 1)], occ_one_send),
        (occ_all.at[pl.ds(0, SIDE - 1)], occ_ring_send),
        (strips.at[pl.ds(0, SIDE - 1)], strip_send),
    ):
        remote(piece, piece, sem, io_sem.at[0], at(0, 1)).wait_send()

    lines = shares.at[pl.ds(0, PLANE - 1)]
    remote(lines, lines, chi_send.at[0], chi_recv.at[0], at(0, 1)).wait()
    shares_rep[pl.ds(rep_ix, 1), :] = jnp.sum(shares[...], axis=0, keepdims=True)
    line = shares_rep.at[pl.ds(rep_ix, 1)]
    for i in range(1, SIDE):
        send(line, line, chi_send.at[1], chi_recv.at[1], (grid_ix, around(rep_ix, i)))
    blocks = vir_back.at[pl.ds(0, SIDE - 1)]
    remote(blocks, blocks, swap_send.at[2], swap_recv.at[2], at(0, 1)).wait()
    for j in range(1, SIDE):
        for a in range(SIDE):
            vir_out[0, :, tile_of(a * sa + part_b[j])] = vir_back[j, :, a * TILE : (a + 1) * TILE]
    pair_occ.wait()
    for i in range(SIDE):
        for m in range(HALF):
            rows = rows_of(part_a[i] + (2 * m + 1 - par) * sb)
            occ_out[0, rows, :] = occ_back[(i * HALF + m) * ROWS : (i * HALF + m + 1) * ROWS]
    lines = shares_rep.at[pl.ds(0, SIDE - 1)]
    remote(lines, lines, chi_send.at[1], chi_recv.at[1], (grid_ix, around(rep_ix, 1))).wait()
    share = jnp.sum(shares_rep[...], axis=0, keepdims=True) * scale
    share = fold(jnp.where(spot, jnp.broadcast_to(share, (RB, TILE)), 0.0))
    chi_out[...] = share[:, :RB]


def write_out(occ_ref, vir_ref, chi_ref, occ_out, vir_out, chi_out, sems):
    copies = [
        pltpu.make_async_copy(src, dst, sems.at[i])
        for i, (src, dst) in enumerate(((occ_ref, occ_out), (vir_ref, vir_out), (chi_ref, chi_out)))
    ]
    for copy in copies:
        copy.start()
    for copy in copies:
        copy.wait()


def per_device(b_tensor, green_occ, green_vir, b_pattern, g_pattern):
    scale = -1.0 / (ORBS * math.sqrt(lax.axis_size("rep")))
    vmem = pl.BlockSpec(memory_space=pltpu.VMEM)
    hbm = pl.BlockSpec(memory_space=pltpu.HBM)
    dma = pltpu.SemaphoreType.DMA
    shapes = (
        jax.ShapeDtypeStruct((1, ORBS, TILE), BF16),
        jax.ShapeDtypeStruct((1, ROWS, ORBS * RB), BF16),
        jax.ShapeDtypeStruct((RB, RB), F32),
    )
    arguments = [
        pltpu.with_memory_space_constraint(t, pltpu.HBM)
        for t in (b_tensor, green_occ, green_vir, b_pattern, g_pattern)
    ]
    results = pl.pallas_call(
        functools.partial(kernel, scale),
        out_shape=shapes,
        in_specs=[hbm] * 5,
        out_specs=(vmem, vmem, vmem),
        scratch_shapes=[
            pltpu.VMEM(b_tensor.shape, BF16),
            pltpu.VMEM(green_occ.shape, BF16),
            pltpu.VMEM(green_vir.shape, BF16),
            pltpu.SMEM(b_pattern.shape, jnp.int32),
            pltpu.SMEM(g_pattern.shape, jnp.int32),
            pltpu.VMEM((SIDE, ROWS, 128), BF16),
            pltpu.VMEM((SIDE, SIDE, ROWS, 128), BF16),
            pltpu.VMEM((SIDE, HALF, ROWS, ORBS), BF16),
            pltpu.VMEM((SIDE, SIDE, ROWS, WIDE), BF16),
            pltpu.VMEM((SIDE, 128, ORBS), BF16),
            pltpu.VMEM((SIDE, SIDE, ROWS, 2 * TILE), BF16),
            pltpu.VMEM((ORBS, 2 * TILE), BF16),
            pltpu.VMEM((WIDE, WIDE), BF16),
            pltpu.VMEM((128, WIDE), BF16),
            pltpu.VMEM((128, WIDE), BF16),
            pltpu.VMEM((2 * SIDE, 64, TILE), BF16),
            pltpu.VMEM((SIDE, ROWS, WIDE), BF16),
            pltpu.VMEM((512, 2 * TILE), BF16),
            pltpu.VMEM((512, TILE), BF16),
            pltpu.VMEM((512, TILE), BF16),
            pltpu.VMEM((PLANE, TILE), F32),
            pltpu.VMEM((SIDE, TILE), F32),
            dma((5,)),
            dma((2,)),
            dma((2,)),
            dma,
            dma((2,)),
            dma,
            dma((2, 7)),
            dma,
            dma((2, 3 * SUBS + SUBS // 2)),
            dma((4,)),
            dma((4,)),
            dma((2,)),
            dma((2,)),
        ],
        compiler_params=pltpu.CompilerParams(
            collective_id=0, has_side_effects=True, vmem_limit_bytes=40 * 1024 * 1024
        ),
        cost_estimate=pl.CostEstimate(flops=600_000_000, bytes_accessed=1_200_000, transcendentals=0),
    )(*arguments)
    return pl.pallas_call(
        write_out,
        out_shape=shapes,
        in_specs=[vmem] * 3,
        out_specs=(hbm,) * 3,
        scratch_shapes=[dma((3,))],
        compiler_params=pltpu.CompilerParams(has_side_effects=True),
    )(*results)


def solution(mesh):
    return jax.shard_map(
        per_device,
        mesh=mesh,
        in_specs=(
            P("rep", "grid", None),
            P("rep", "grid", None),
            P("rep", "grid", None),
            P("rep", None, None),
            P("rep", None, None),
        ),
        out_specs=(P("rep", None, "grid"), P("rep", "grid", None), P()),
        check_vma=False,
    )
```

```python
import functools
import math

import jax
import jax.numpy as jnp
from jax import lax
from jax.experimental import pallas as pl
from jax.experimental.pallas import tpu as pltpu
from jax.sharding import PartitionSpec as P

MESH = pl.DeviceIdType.MESH
SIDE = 8
PLANE = SIDE * SIDE
HALF = SIDE // 2
ROWS = 16
ORBS = 1024
RB = 8
TILE = ROWS * RB
WIDE = SIDE * TILE
F32 = jnp.float32
BF16 = jnp.bfloat16


def around(index, step):
    return lax.rem(index + (step + SIDE), SIDE)


FAR = [4, 5, 3, 6, 2, 7, 1]
SUBS = 4


def kernel(
    scale,
    b_hbm,
    occ_hbm,
    vir_hbm,
    bp_hbm,
    gp_hbm,
    occ_out,
    vir_out,
    chi_out,
    b_ref,
    occ_ref,
    vir_ref,
    bp_ref,
    gp_ref,
    vir_own,
    vir_all,
    occ_all,
    strips,
    left_side,
    landed,
    both,
    perm,
    mixed,
    merged,
    vir_land,
    vir_back,
    occ_pair,
    occ_two,
    occ_back,
    shares,
    shares_rep,
    io_sem,
    vir_send,
    vir_recv,
    occ_one_send,
    occ_one_recv,
    occ_ring_send,
    occ_ring_recv,
    strip_send,
    strip_recv,
    swap_send,
    swap_recv,
    chi_send,
    chi_recv,
):
    grid_ix = lax.axis_index("grid")
    rep_ix = lax.axis_index("rep")
    z, y = grid_ix // SIDE, grid_ix % SIDE
    core = rep_ix % 2
    a0 = z + core * (y - z)
    b0 = y + core * (z - y)
    sa = SIDE - (SIDE - 1) * core
    sb = 1 + (SIDE - 1) * core
    par = b0 % 2
    jb = b0 // 2
    mate = around(b0, 1 - 2 * par)
    abs_a = [around(a0, i) for i in range(SIDE)]
    abs_b = [around(b0, j) for j in range(SIDE)]
    part_a = [a * sa for a in abs_a]
    part_b = [b * sb for b in abs_b]

    def nat(i, j):
        return part_a[i % SIDE] + part_b[j % SIDE]

    def at(i, j):
        return (nat(i, j), rep_ix)

    def at_mate(i):
        return (part_a[i % SIDE] + mate * sb, rep_ix)

    def remote(src, dst, send, recv, where):
        return pltpu.make_async_remote_copy(
            src_ref=src, dst_ref=dst, send_sem=send, recv_sem=recv, device_id=where, device_id_type=MESH
        )

    def send(*copy):
        remote(*copy).start()

    def tile_of(i):
        return pl.ds(pl.multiple_of(i * TILE, TILE), TILE)

    def rows_of(i, count=ROWS):
        return pl.ds(pl.multiple_of(i * count, count), count)

    barrier = pltpu.get_barrier_semaphore()
    for i in range(1, SIDE):
        for where in (at(i, 0), at(0, i), (grid_ix, around(rep_ix, i))):
            pl.semaphore_signal(barrier, inc=1, device_id=where, device_id_type=MESH)

    loads = [
        pltpu.make_async_copy(src, dst, io_sem.at[i])
        for i, (src, dst) in enumerate(
            ((gp_hbm, gp_ref), (vir_hbm, vir_ref), (bp_hbm, bp_ref), (b_hbm, b_ref), (occ_hbm, occ_ref))
        )
    ]
    for load in loads:
        load.start()

    molecule = grid_ix // 4
    lane = lax.broadcasted_iota(jnp.int32, (ROWS, 128), 1)
    loads[0].wait()
    loads[1].wait()
    keeps = [
        jnp.where(lane < 64, gp_ref[0, molecule, 2 * t], gp_ref[0, molecule, 2 * t + 1]).astype(F32)
        for t in range(SIDE)
    ]
    tiles = [vir_ref[0, :, t * 128 : (t + 1) * 128].astype(F32) * keeps[t] for t in range(SIDE)]
    for bit in (1, 2, 4):
        high = (lane // ROWS // bit) % 2 + 2 * core
        for t in range(SIDE):
            if t & bit == 0:
                u = t + bit
                low_tile = jnp.where(high == 1, pltpu.roll(tiles[u], ROWS * bit, 1), tiles[t])
                high_tile = jnp.where(high == 0, pltpu.roll(tiles[t], 128 - ROWS * bit, 1), tiles[u])
                tiles[t], tiles[u] = low_tile, high_tile
    for b in range(SIDE):
        vir_own[b] = tiles[b].astype(BF16)
    vir_all[0, b0] = vir_own[b0]

    loads[2].wait()
    loads[3].wait()
    for m in range(2 * SIDE):
        keep = jnp.full((ROWS, 512), bp_ref[0, molecule, m], jnp.int32).astype(F32).astype(BF16)
        cols = slice(m * 512, (m + 1) * 512)
        b_ref[0, :, cols] = b_ref[0, :, cols] * keep
    for i in range(SIDE):
        for b in range(SIDE):
            strips[0, i, :, b * TILE : (b + 1) * TILE] = b_ref[0, :, tile_of(part_a[i] + b * sb)]
    loads[4].wait()
    for t in range(SIDE):
        cols = slice(t * 128, (t + 1) * 128)
        occ_all[0, 0, :, cols] = occ_ref[0, :, cols] * keeps[t].astype(BF16)

    pl.semaphore_wait(barrier, 3 * (SIDE - 1))

    for j in FAR:
        send(vir_own.at[abs_b[j]], vir_all.at[0, b0], vir_send.at[0], vir_recv.at[0], at(0, j))

    def strip_ring(way, d, u):
        sign = 1 - 2 * way
        send(
            strips.at[-sign * (d - 1) % SIDE, pl.ds(2 * u, 2)],
            strips.at[-sign * d % SIDE, pl.ds(2 * u, 2)],
            strip_send,
            strip_recv.at[way, SUBS * (d - 1) + u % (SUBS if d < 4 else SUBS // 2)],
            at(0, sign),
        )

    def strip_wait(way, d, u):
        piece = strips.at[(2 * way - 1) * d % SIDE, pl.ds(2 * u, 2)]
        slot = strip_recv.at[way, SUBS * (d - 1) + u % (SUBS if d < 4 else SUBS // 2)]
        remote(piece, piece, strip_send, slot, at(0, 1)).wait_recv()

    def occ_ring(way, d, g):
        sign = 1 - 2 * way
        send(
            occ_all.at[-sign * (d - 1) % SIDE, pl.ds(2 * g, 2)],
            occ_all.at[-sign * d % SIDE, pl.ds(2 * g, 2)],
            occ_ring_send,
            occ_ring_recv.at[way, 2 * (d - 1) + g if d < 4 else 6],
            at(sign, 0),
        )

    def occ_step(d):
        for g in range(2):
            for way in range(2):
                if d == 4 and g != way:
                    continue
                piece = occ_all.at[(2 * way - 1) * d % SIDE, pl.ds(2 * g, 2)]
                slot = occ_ring_recv.at[way, 2 * (d - 1) + g if d < 4 else 6]
                remote(piece, piece, occ_ring_send, slot, at(1, 0)).wait_recv()
                if d < 3 or (d == 3 and g == way):
                    occ_ring(way, d + 1, g)

    def swap(j):
        pair = pl.ds(pl.multiple_of(jb * 2 * TILE, 2 * TILE), 2 * TILE)
        for i in FAR:
            send(strips.at[j, i, :, pair], landed.at[-i % SIDE, j], swap_send.at[0], swap_recv.at[0], at(i, 0))
        landed[0, j] = strips[j, 0, :, pair]

    def fill(i, carry):
        target = lax.broadcasted_iota(jnp.int32, (256, WIDE), 1)
        target = (target % 128) * RB + target // 128
        row = lax.broadcasted_iota(jnp.int32, (256, WIDE), 0) + i * 256
        perm[pl.ds(pl.multiple_of(i * 256, 256), 256), :] = jnp.where(row == target, 1.0, 0.0).astype(BF16)
        return carry

    def part(j):
        apart = jnp.dot(strips[j].reshape(128, WIDE), perm[...], preferred_element_type=F32).astype(BF16)
        for i in range(SIDE):
            for q in range(RB):
                left_side[j, q * ROWS : (q + 1) * ROWS, i * 128 : (i + 1) * 128] = apart[
                    i * ROWS : (i + 1) * ROWS, q * 128 : (q + 1) * 128
                ]

    place = [((par + j) % 2) * HALF + abs_b[j] // 2 for j in range(SIDE)]

    def contract(j):
        product = jnp.dot(left_side[j], vir_all[...].reshape(ORBS, 128), preferred_element_type=F32).astype(BF16)
        for q in range(RB):
            mixed[rows_of(place[j]), q * 128 : (q + 1) * 128] = product[q * ROWS : (q + 1) * ROWS]

    for m in (2, 1, 3):
        send(occ_all.at[0, 0], occ_all.at[0, -m % HALF], occ_one_send, occ_one_recv.at[-m % HALF // 2], at(0, 2 * m))
    for u in range(SUBS):
        for way in range(2):
            strip_ring(way, 1, u)
    swap(0)
    lax.fori_loop(0, WIDE // 256, fill, 0)

    blocks = vir_all.at[0, pl.ds(0, SIDE - 1)]
    remote(blocks, blocks, vir_send.at[0], vir_recv.at[0], at(0, 1)).wait()
    def vir_ring(way, d):
        sign = 1 - 2 * way
        part_of = slice(None) if d < 4 else pl.ds(way * HALF, HALF)
        send(
            vir_all.at[-sign * (d - 1) % SIDE, part_of],
            vir_all.at[-sign * d % SIDE, part_of],
            vir_send.at[1],
            vir_recv.at[2 * d - 1 + way],
            at(sign, 0),
        )

    def vir_step(d):
        for way in range(2):
            part_of = slice(None) if d < 4 else pl.ds(way * HALF, HALF)
            chunk = vir_all.at[(2 * way - 1) * d % SIDE, part_of]
            remote(chunk, chunk, vir_send.at[1], vir_recv.at[2 * d - 1 + way], at(1, 0)).wait_recv()
            if d < 4:
                vir_ring(way, d + 1)

    for way in range(2):
        vir_ring(way, 1)

    def occ_begin():
        for g in range(2):
            blocks = occ_all.at[0, pl.ds(2, 2)] if g else occ_all.at[0, pl.ds(1, 1)]
            remote(blocks, blocks, occ_one_send, occ_one_recv.at[g], at(0, 1)).wait_recv()
            for way in range(2):
                occ_ring(way, 1, g)

    def vir_end():
        vir_step(4)
        chunks = vir_all.at[pl.ds(0, SIDE - 1)]
        remote(chunks, chunks, vir_send.at[1], vir_recv.at[1], at(1, 0)).wait_send()

    def run(*steps):
        return [functools.partial(*step) for step in steps]

    work = {
        (1, 0): run((part, 0)),
        (1, 2): run((occ_begin,)),
        (2, 0): run((vir_step, 1), (swap, 1), (swap, 7)),
        (2, 1): run((part, 1)),
        (2, 2): run((part, 7)),
        (2, 3): run((vir_step, 2), (occ_step, 1)),
        (3, 0): run((swap, 2), (swap, 6)),
        (3, 1): run((vir_step, 3), (part, 2)),
        (3, 2): run((part, 6)),
        (3, 3): run((occ_step, 2),),
        (4, 0): run((swap, 3), (swap, 5), (part, 3)),
        (4, 1): run((part, 5), (vir_end,), (contract, 0), (contract, 1), (contract, 7), (contract, 2), (contract, 6), (contract, 3), (contract, 5)),
    }
    for d in range(1, 5):
        for u in range(SUBS if d < 4 else SUBS // 2):
            for way in range(2):
                sub = u if d < 4 else u + way * SUBS // 2
                strip_wait(way, d, sub)
                if d < 3 or (d == 3 and u // (SUBS // 2) == way):
                    strip_ring(way, d + 1, sub)
            for step in work.get((d, u), ()):
                step()
    swap(4)
    part(4)
    contract(4)

    merged[...] = lax.dot_general(
        mixed[...], perm[...], (((1,), (1,)), ((), ())), preferred_element_type=F32
    ).astype(BF16)

    for i in FAR + [0]:
        for own in (False, True):
            if not (own and i == 0):
                parity = par if own else 1 - par
                send(
                    merged.at[rows_of(parity, 64), tile_of(abs_a[i])],
                    vir_land.at[par * SIDE + -i % SIDE],
                    swap_send.at[1],
                    swap_recv.at[1],
                    at(i, 0) if own else at_mate(i),
                )
    vir_land[par * SIDE] = merged[rows_of(par, 64), tile_of(a0)]

    for j in FAR:
        send(merged.at[rows_of(place[j])], vir_back.at[-j % SIDE], swap_send.at[2], swap_recv.at[2], at(0, j))
    occ_step(3)
    pieces = landed.at[pl.ds(0, SIDE - 1)]
    remote(pieces, pieces, swap_send.at[0], swap_recv.at[0], at(1, 0)).wait()
    for i in range(SIDE):
        for j in range(SIDE):
            both[rows_of(nat(i, j)), :] = landed[i, j]

    turn = [lax.rem(jb + m, HALF) for m in range(HALF)]

    def put_occ(i):
        product = jnp.dot(occ_all[i].reshape(64, ORBS), both[...], preferred_element_type=F32).astype(BF16)
        for m in range(HALF):
            occ_pair[rows_of(i * HALF + turn[m]), :] = product[m * ROWS : (m + 1) * ROWS]

    for i in (0, 1, 7, 2, 6, 3, 5):
        put_occ(i)
    occ_step(4)
    put_occ(4)
    occ_two[...] = occ_pair[:, tile_of(1 - par)]

    most = vir_land.at[pl.ds(0, 2 * SIDE - 1)]
    remote(most, most, swap_send.at[1], swap_recv.at[1], at(1, 0)).wait()

    gram = jnp.zeros((TILE, TILE), F32)
    for c in range(2):
        mine = occ_pair[:, c * TILE : (c + 1) * TILE]
        theirs = vir_land[c * SIDE : (c + 1) * SIDE].reshape(512, TILE)
        gram += lax.dot_general(mine, theirs, (((0,), (0,)), ((), ())), preferred_element_type=F32)
    row = lax.broadcasted_iota(jnp.int32, (TILE, TILE), 0)
    col = lax.broadcasted_iota(jnp.int32, (TILE, TILE), 1)
    gram = jnp.where(row // RB == col // RB, gram, 0.0)
    share = jnp.sum(gram.reshape(ROWS, RB, TILE), axis=0)

    def fold(values):
        for shift in (8, 16, 32, 64):
            values = values + pltpu.roll(values, shift, 1)
        return values

    spot = lax.broadcasted_iota(jnp.int32, (RB, TILE), 1) // RB == lax.broadcasted_iota(jnp.int32, (RB, TILE), 0)
    share = jnp.sum(jnp.where(spot, fold(share), 0.0), axis=0, keepdims=True)
    shares_rep[pl.ds(rep_ix, 1), :] = share
    line = shares_rep.at[pl.ds(rep_ix, 1)]
    for i in range(1, SIDE):
        send(line, line, chi_send.at[1], chi_recv.at[1], (grid_ix, around(rep_ix, i)))

    pair_occ = remote(occ_two, occ_back, swap_send.at[3], swap_recv.at[3], at_mate(0))
    pair_occ.start()

    lines = shares_rep.at[pl.ds(0, SIDE - 1)]
    remote(lines, lines, chi_send.at[1], chi_recv.at[1], (grid_ix, around(rep_ix, 1))).wait()
    shares[pl.ds(grid_ix, 1), :] = jnp.sum(shares_rep[...], axis=0, keepdims=True)
    line = shares.at[pl.ds(grid_ix, 1)]
    for i in FAR + [0]:
        for j in FAR + [0]:
            if (i, j) != (0, 0):
                send(line, line, chi_send.at[0], chi_recv.at[0], at(i, j))

    for a in range(SIDE):
        vir_out[0, :, tile_of(a * sa + part_b[0])] = merged[rows_of(place[0]), a * TILE : (a + 1) * TILE]
    for i in range(SIDE):
        for m in range(HALF):
            rows = rows_of(part_a[i] + (2 * m + par) * sb)
            occ_out[0, rows, :] = occ_pair[(i * HALF + m) * ROWS : (i * HALF + m + 1) * ROWS, tile_of(par)]
    for piece, sem in (
        (occ_all.at[0, pl.ds(0, HALF - 1)], occ_one_send),
        (occ_all.at[pl.ds(0, SIDE - 1)], occ_ring_send),
        (strips.at[pl.ds(0, SIDE - 1)], strip_send),
    ):
        remote(piece, piece, sem, io_sem.at[0], at(0, 1)).wait_send()

    blocks = vir_back.at[pl.ds(0, SIDE - 1)]
    remote(blocks, blocks, swap_send.at[2], swap_recv.at[2], at(0, 1)).wait()
    for j in range(1, SIDE):
        for a in range(SIDE):
            vir_out[0, :, tile_of(a * sa + part_b[j])] = vir_back[j, :, a * TILE : (a + 1) * TILE]
    pair_occ.wait()
    for i in range(SIDE):
        for m in range(HALF):
            rows = rows_of(part_a[i] + (2 * m + 1 - par) * sb)
            occ_out[0, rows, :] = occ_back[(i * HALF + m) * ROWS : (i * HALF + m + 1) * ROWS]
    lines = shares.at[pl.ds(0, PLANE - 1)]
    remote(lines, lines, chi_send.at[0], chi_recv.at[0], at(0, 1)).wait()
    share = jnp.sum(shares[...], axis=0, keepdims=True) * scale
    share = fold(jnp.where(spot, jnp.broadcast_to(share, (RB, TILE)), 0.0))
    chi_out[...] = share[:, :RB]


def per_device(b_tensor, green_occ, green_vir, b_pattern, g_pattern):
    scale = -1.0 / (ORBS * math.sqrt(lax.axis_size("rep")))
    vmem = pl.BlockSpec(memory_space=pltpu.VMEM)
    hbm = pl.BlockSpec(memory_space=pltpu.HBM)
    dma = pltpu.SemaphoreType.DMA
    shapes = (
        jax.ShapeDtypeStruct((1, ORBS, TILE), BF16),
        jax.ShapeDtypeStruct((1, ROWS, ORBS * RB), BF16),
        jax.ShapeDtypeStruct((RB, RB), F32),
    )
    arguments = [
        pltpu.with_memory_space_constraint(t, pltpu.HBM)
        for t in (b_tensor, green_occ, green_vir, b_pattern, g_pattern)
    ]
    return pl.pallas_call(
        functools.partial(kernel, scale),
        out_shape=shapes,
        in_specs=[hbm] * 5,
        out_specs=(vmem, vmem, vmem),
        scratch_shapes=[
            pltpu.VMEM(b_tensor.shape, BF16),
            pltpu.VMEM(green_occ.shape, BF16),
            pltpu.VMEM(green_vir.shape, BF16),
            pltpu.SMEM(b_pattern.shape, jnp.int32),
            pltpu.SMEM(g_pattern.shape, jnp.int32),
            pltpu.VMEM((SIDE, ROWS, 128), BF16),
            pltpu.VMEM((SIDE, SIDE, ROWS, 128), BF16),
            pltpu.VMEM((SIDE, HALF, ROWS, ORBS), BF16),
            pltpu.VMEM((SIDE, SIDE, ROWS, WIDE), BF16),
            pltpu.VMEM((SIDE, 128, ORBS), BF16),
            pltpu.VMEM((SIDE, SIDE, ROWS, 2 * TILE), BF16),
            pltpu.VMEM((ORBS, 2 * TILE), BF16),
            pltpu.VMEM((WIDE, WIDE), BF16),
            pltpu.VMEM((128, WIDE), BF16),
            pltpu.VMEM((128, WIDE), BF16),
            pltpu.VMEM((2 * SIDE, 64, TILE), BF16),
            pltpu.VMEM((SIDE, ROWS, WIDE), BF16),
            pltpu.VMEM((512, 2 * TILE), BF16),
            pltpu.VMEM((512, TILE), BF16),
            pltpu.VMEM((512, TILE), BF16),
            pltpu.VMEM((PLANE, TILE), F32),
            pltpu.VMEM((SIDE, TILE), F32),
            dma((5,)),
            dma((2,)),
            dma((9,)),
            dma,
            dma((2,)),
            dma,
            dma((2, 7)),
            dma,
            dma((2, 3 * SUBS + SUBS // 2)),
            dma((4,)),
            dma((4,)),
            dma((2,)),
            dma((2,)),
        ],
        compiler_params=pltpu.CompilerParams(
            collective_id=0, has_side_effects=True, vmem_limit_bytes=40 * 1024 * 1024
        ),
        cost_estimate=pl.CostEstimate(flops=600_000_000, bytes_accessed=1_200_000, transcendentals=0),
    )(*arguments)


def solution(mesh):
    return jax.shard_map(
        per_device,
        mesh=mesh,
        in_specs=(
            P("rep", "grid", None),
            P("rep", "grid", None),
            P("rep", "grid", None),
            P("rep", None, None),
            P("rep", None, None),
        ),
        out_specs=(P("rep", None, "grid"), P("rep", "grid", None), P()),
        check_vma=False,
    )
```

```python
import functools
import math

import jax
import jax.numpy as jnp
from jax import lax
from jax.experimental import pallas as pl
from jax.experimental.pallas import tpu as pltpu
from jax.sharding import PartitionSpec as P

MESH = pl.DeviceIdType.MESH
SIDE = 8
PLANE = SIDE * SIDE
HALF = SIDE // 2
ROWS = 16
ORBS = 1024
RB = 8
TILE = ROWS * RB
WIDE = SIDE * TILE
F32 = jnp.float32
BF16 = jnp.bfloat16


def around(index, step):
    return lax.rem(index + (step + SIDE), SIDE)


FAR = [4, 5, 3, 6, 2, 7, 1]
ORDER = [0, 1, 7, 2, 6, 3, 5, 4]
SUBS = 4


def kernel(
    scale,
    b_hbm,
    occ_hbm,
    vir_hbm,
    bp_hbm,
    gp_hbm,
    occ_out,
    vir_out,
    chi_out,
    b_ref,
    occ_ref,
    vir_ref,
    bp_ref,
    gp_ref,
    vir_own,
    vir_all,
    occ_all,
    strips,
    left_side,
    landed,
    both,
    perm,
    mixed,
    merged,
    vir_land,
    vir_back,
    occ_pair,
    occ_two,
    occ_back,
    shares,
    shares_rep,
    io_sem,
    vir_send,
    vir_recv,
    occ_one_send,
    occ_one_recv,
    occ_ring_send,
    occ_ring_recv,
    strip_send,
    strip_recv,
    swap_send,
    swap_recv,
    chi_send,
    chi_recv,
):
    grid_ix = lax.axis_index("grid")
    rep_ix = lax.axis_index("rep")
    z, y = grid_ix // SIDE, grid_ix % SIDE
    core = rep_ix % 2
    a0 = z + core * (y - z)
    b0 = y + core * (z - y)
    sa = SIDE - (SIDE - 1) * core
    sb = 1 + (SIDE - 1) * core
    par = b0 % 2
    jb = b0 // 2
    mate = around(b0, 1 - 2 * par)
    abs_a = [around(a0, i) for i in range(SIDE)]
    abs_b = [around(b0, j) for j in range(SIDE)]
    part_a = [a * sa for a in abs_a]
    part_b = [b * sb for b in abs_b]

    def nat(i, j):
        return part_a[i % SIDE] + part_b[j % SIDE]

    def at(i, j):
        return (nat(i, j), rep_ix)

    def at_mate(i):
        return (part_a[i % SIDE] + mate * sb, rep_ix)

    def remote(src, dst, send, recv, where):
        return pltpu.make_async_remote_copy(
            src_ref=src, dst_ref=dst, send_sem=send, recv_sem=recv, device_id=where, device_id_type=MESH
        )

    def send(*copy):
        remote(*copy).start()

    def tile_of(i):
        return pl.ds(pl.multiple_of(i * TILE, TILE), TILE)

    def rows_of(i, count=ROWS):
        return pl.ds(pl.multiple_of(i * count, count), count)

    barrier = pltpu.get_barrier_semaphore()
    for i in range(1, SIDE):
        for where in (at(i, 0), at(0, i), (grid_ix, around(rep_ix, i))):
            pl.semaphore_signal(barrier, inc=1, device_id=where, device_id_type=MESH)

    loads = [
        pltpu.make_async_copy(src, dst, io_sem.at[i])
        for i, (src, dst) in enumerate(
            ((gp_hbm, gp_ref), (vir_hbm, vir_ref), (bp_hbm, bp_ref), (b_hbm, b_ref), (occ_hbm, occ_ref))
        )
    ]
    for load in loads:
        load.start()

    molecule = grid_ix // 4
    lane = lax.broadcasted_iota(jnp.int32, (ROWS, 128), 1)
    loads[0].wait()
    loads[1].wait()
    keeps = [
        jnp.where(lane < 64, gp_ref[0, molecule, 2 * t], gp_ref[0, molecule, 2 * t + 1]).astype(F32)
        for t in range(SIDE)
    ]
    tiles = [vir_ref[0, :, t * 128 : (t + 1) * 128].astype(F32) * keeps[t] for t in range(SIDE)]
    for bit in (1, 2, 4):
        high = (lane // ROWS // bit) % 2 + 2 * core
        for t in range(SIDE):
            if t & bit == 0:
                u = t + bit
                low_tile = jnp.where(high == 1, pltpu.roll(tiles[u], ROWS * bit, 1), tiles[t])
                high_tile = jnp.where(high == 0, pltpu.roll(tiles[t], 128 - ROWS * bit, 1), tiles[u])
                tiles[t], tiles[u] = low_tile, high_tile
    for b in range(SIDE):
        vir_own[b] = tiles[b].astype(BF16)
    vir_all[0, b0] = vir_own[b0]

    loads[2].wait()
    loads[3].wait()
    for m in range(2 * SIDE):
        keep = jnp.full((ROWS, 512), bp_ref[0, molecule, m], jnp.int32).astype(F32).astype(BF16)
        cols = slice(m * 512, (m + 1) * 512)
        b_ref[0, :, cols] = b_ref[0, :, cols] * keep
    for i in range(SIDE):
        for b in range(SIDE):
            strips[0, i, :, b * TILE : (b + 1) * TILE] = b_ref[0, :, tile_of(part_a[i] + b * sb)]
    loads[4].wait()
    for t in range(SIDE):
        cols = slice(t * 128, (t + 1) * 128)
        occ_all[0, 0, :, cols] = occ_ref[0, :, cols] * keeps[t].astype(BF16)

    pl.semaphore_wait(barrier, 3 * (SIDE - 1))

    for j in FAR:
        send(vir_own.at[abs_b[j]], vir_all.at[0, b0], vir_send.at[0], vir_recv.at[0], at(0, j))

    def strip_ring(way, d, u):
        sign = 1 - 2 * way
        send(
            strips.at[-sign * (d - 1) % SIDE, pl.ds(2 * u, 2)],
            strips.at[-sign * d % SIDE, pl.ds(2 * u, 2)],
            strip_send,
            strip_recv.at[way, SUBS * (d - 1) + u % (SUBS if d < 4 else SUBS // 2)],
            at(0, sign),
        )

    def strip_wait(way, d, u):
        piece = strips.at[(2 * way - 1) * d % SIDE, pl.ds(2 * u, 2)]
        slot = strip_recv.at[way, SUBS * (d - 1) + u % (SUBS if d < 4 else SUBS // 2)]
        remote(piece, piece, strip_send, slot, at(0, 1)).wait_recv()

    def occ_ring(way, d, g):
        sign = 1 - 2 * way
        send(
            occ_all.at[-sign * (d - 1) % SIDE, pl.ds(2 * g, 2)],
            occ_all.at[-sign * d % SIDE, pl.ds(2 * g, 2)],
            occ_ring_send,
            occ_ring_recv.at[way, 2 * (d - 1) + g if d < 4 else 6],
            at(sign, 0),
        )

    def occ_step(d):
        for g in range(2):
            for way in range(2):
                if d == 4 and g != way:
                    continue
                piece = occ_all.at[(2 * way - 1) * d % SIDE, pl.ds(2 * g, 2)]
                slot = occ_ring_recv.at[way, 2 * (d - 1) + g if d < 4 else 6]
                remote(piece, piece, occ_ring_send, slot, at(1, 0)).wait_recv()
                if d < 3 or (d == 3 and g == way):
                    occ_ring(way, d + 1, g)

    def swap(j):
        pair = pl.ds(pl.multiple_of(jb * 2 * TILE, 2 * TILE), 2 * TILE)
        for i in FAR:
            send(strips.at[j, i, :, pair], landed.at[-i % SIDE, j], swap_send.at[0], swap_recv.at[0], at(i, 0))
        landed[0, j] = strips[j, 0, :, pair]

    def fill(i, carry):
        target = lax.broadcasted_iota(jnp.int32, (256, WIDE), 1)
        target = (target % 128) * RB + target // 128
        row = lax.broadcasted_iota(jnp.int32, (256, WIDE), 0) + i * 256
        perm[pl.ds(pl.multiple_of(i * 256, 256), 256), :] = jnp.where(row == target, 1.0, 0.0).astype(BF16)
        return carry

    def part(j):
        apart = jnp.dot(strips[j].reshape(128, WIDE), perm[...], preferred_element_type=F32).astype(BF16)
        for i in range(SIDE):
            for q in range(RB):
                left_side[j, q * ROWS : (q + 1) * ROWS, i * 128 : (i + 1) * 128] = apart[
                    i * ROWS : (i + 1) * ROWS, q * 128 : (q + 1) * 128
                ]

    def contract(j):
        product = jnp.dot(left_side[j], vir_all[...].reshape(ORBS, 128), preferred_element_type=F32).astype(BF16)
        row = ORDER.index(j) * ROWS
        for q in range(RB):
            mixed[row : row + ROWS, q * 128 : (q + 1) * 128] = product[q * ROWS : (q + 1) * ROWS]

    def finish(*js):
        first = ORDER.index(js[0]) * ROWS
        rows = slice(first, first + len(js) * ROWS)
        merged[rows] = lax.dot_general(
            mixed[rows], perm[...], (((1,), (1,)), ((), ())), preferred_element_type=F32
        ).astype(BF16)
        for j in js:
            row = ORDER.index(j) * ROWS
            line = rows_of(abs_b[j] // 2)
            for i in FAR + [0]:
                piece = merged.at[row : row + ROWS, tile_of(abs_a[i])]
                land = vir_land.at[par * SIDE + -i % SIDE, line]
                if j % 2 == 1 or i != 0:
                    send(piece, land, swap_send.at[1], swap_recv.at[1], at_mate(i) if j % 2 else at(i, 0))
            if j % 2 == 0:
                vir_land[par * SIDE, line] = merged[row : row + ROWS, tile_of(a0)]
        for j in js:
            if j != 0:
                row = ORDER.index(j) * ROWS
                send(merged.at[row : row + ROWS], vir_back.at[-j % SIDE], swap_send.at[2], swap_recv.at[2], at(0, j))

    for m in (2, 1, 3):
        send(occ_all.at[0, 0], occ_all.at[0, -m % HALF], occ_one_send, occ_one_recv.at[-m % HALF // 2], at(0, 2 * m))
    for u in range(SUBS):
        for way in range(2):
            strip_ring(way, 1, u)
    swap(0)
    lax.fori_loop(0, WIDE // 256, fill, 0)

    blocks = vir_all.at[0, pl.ds(0, SIDE - 1)]
    remote(blocks, blocks, vir_send.at[0], vir_recv.at[0], at(0, 1)).wait()
    for d in (2, 1):
        for way in range(2):
            step = d * (1 - 2 * way)
            send(vir_all.at[0], vir_all.at[-step % SIDE], vir_send.at[1], vir_recv.at[1 if d == 1 else 2 + way], at(step, 0))

    def vir_relay():
        for way in range(2):
            sign = 1 - 2 * way
            chunk = vir_all.at[-2 * sign % SIDE]
            remote(chunk, chunk, vir_send.at[1], vir_recv.at[2 + way], at(1, 0)).wait_recv()
            half = pl.ds(way * HALF, HALF)
            send(
                vir_all.at[-2 * sign % SIDE, half],
                vir_all.at[HALF, half],
                vir_send.at[1],
                vir_recv.at[1],
                at(2 * sign, 0),
            )
            send(chunk, vir_all.at[-3 * sign % SIDE], vir_send.at[1], vir_recv.at[1], at(sign, 0))

    def occ_begin():
        for g in range(2):
            blocks = occ_all.at[0, pl.ds(2, 2)] if g else occ_all.at[0, pl.ds(1, 1)]
            remote(blocks, blocks, occ_one_send, occ_one_recv.at[g], at(0, 1)).wait_recv()
            for way in range(2):
                occ_ring(way, 1, g)

    def vir_end():
        chunks = vir_all.at[pl.ds(0, 5)]
        remote(chunks, chunks, vir_send.at[1], vir_recv.at[1], at(1, 0)).wait_recv()
        chunks = vir_all.at[pl.ds(0, SIDE - 1)]
        remote(chunks, chunks, vir_send.at[1], vir_recv.at[1], at(1, 0)).wait_send()

    def run(*steps):
        return [functools.partial(*step) for step in steps]

    work = {
        (1, 0): run((part, 0,)),
        (1, 2): run((occ_begin,)),
        (1, 3): run((vir_relay,)),
        (2, 0): run((swap, 1,), (swap, 7,)),
        (2, 1): run((part, 1,)),
        (2, 2): run((part, 7,)),
        (2, 3): run((occ_step, 1,)),
        (3, 0): run((swap, 2,), (swap, 6,)),
        (3, 1): run((part, 2,), (vir_end,), (contract, 0,), (contract, 1,)),
        (3, 2): run((part, 6,), (contract, 7,), (contract, 2,), (contract, 6,)),
        (3, 3): run((occ_step, 2,), (finish, 0, 1, 7, 2, 6,)),
        (4, 0): run((swap, 3,), (swap, 5,), (part, 3,), (contract, 3,)),
        (4, 1): run((part, 5,), (contract, 5,), (finish, 3, 5,)),
    }
    for d in range(1, 5):
        for u in range(SUBS if d < 4 else SUBS // 2):
            for way in range(2):
                sub = u if d < 4 else u + way * SUBS // 2
                strip_wait(way, d, sub)
                if d < 3 or (d == 3 and u // (SUBS // 2) == way):
                    strip_ring(way, d + 1, sub)
            for step in work.get((d, u), ()):
                step()
    swap(4)
    part(4)
    contract(4)

    finish(4)
    occ_step(3)
    pieces = landed.at[pl.ds(0, SIDE - 1)]
    remote(pieces, pieces, swap_send.at[0], swap_recv.at[0], at(1, 0)).wait()
    for i in range(SIDE):
        for j in range(SIDE):
            both[rows_of(nat(i, j)), :] = landed[i, j]

    turn = [lax.rem(jb + m, HALF) for m in range(HALF)]

    def put_occ(i):
        product = jnp.dot(occ_all[i].reshape(64, ORBS), both[...], preferred_element_type=F32).astype(BF16)
        for m in range(HALF):
            occ_pair[rows_of(i * HALF + turn[m]), :] = product[m * ROWS : (m + 1) * ROWS]

    for i in (0, 1, 7, 2, 6, 3, 5):
        put_occ(i)
    occ_step(4)
    put_occ(4)
    occ_two[...] = occ_pair[:, tile_of(1 - par)]

    most = vir_land.at[pl.ds(0, 2 * SIDE - 1)]
    remote(most, most, swap_send.at[1], swap_recv.at[1], at(1, 0)).wait()

    gram = jnp.zeros((TILE, TILE), F32)
    for c in range(2):
        mine = occ_pair[:, c * TILE : (c + 1) * TILE]
        theirs = vir_land[c * SIDE : (c + 1) * SIDE].reshape(512, TILE)
        gram += lax.dot_general(mine, theirs, (((0,), (0,)), ((), ())), preferred_element_type=F32)
    row = lax.broadcasted_iota(jnp.int32, (TILE, TILE), 0)
    col = lax.broadcasted_iota(jnp.int32, (TILE, TILE), 1)
    gram = jnp.where(row // RB == col // RB, gram, 0.0)
    share = jnp.sum(gram.reshape(ROWS, RB, TILE), axis=0)

    def fold(values):
        for shift in (8, 16, 32, 64):
            values = values + pltpu.roll(values, shift, 1)
        return values

    spot = lax.broadcasted_iota(jnp.int32, (RB, TILE), 1) // RB == lax.broadcasted_iota(jnp.int32, (RB, TILE), 0)
    share = jnp.sum(jnp.where(spot, fold(share), 0.0), axis=0, keepdims=True)
    shares_rep[pl.ds(rep_ix, 1), :] = share
    line = shares_rep.at[pl.ds(rep_ix, 1)]
    for i in range(1, SIDE):
        send(line, line, chi_send.at[1], chi_recv.at[1], (grid_ix, around(rep_ix, i)))

    pair_occ = remote(occ_two, occ_back, swap_send.at[3], swap_recv.at[3], at_mate(0))
    pair_occ.start()

    lines = shares_rep.at[pl.ds(0, SIDE - 1)]
    remote(lines, lines, chi_send.at[1], chi_recv.at[1], (grid_ix, around(rep_ix, 1))).wait()
    shares[pl.ds(grid_ix, 1), :] = jnp.sum(shares_rep[...], axis=0, keepdims=True)
    line = shares.at[pl.ds(grid_ix, 1)]
    for i in FAR + [0]:
        for j in FAR + [0]:
            if (i, j) != (0, 0):
                send(line, line, chi_send.at[0], chi_recv.at[0], at(i, j))

    for a in range(SIDE):
        vir_out[0, :, tile_of(a * sa + part_b[0])] = merged[:ROWS, a * TILE : (a + 1) * TILE]
    for i in range(SIDE):
        for m in range(HALF):
            rows = rows_of(part_a[i] + (2 * m + par) * sb)
            occ_out[0, rows, :] = occ_pair[(i * HALF + m) * ROWS : (i * HALF + m + 1) * ROWS, tile_of(par)]
    for piece, sem in (
        (occ_all.at[0, pl.ds(0, HALF - 1)], occ_one_send),
        (occ_all.at[pl.ds(0, SIDE - 1)], occ_ring_send),
        (strips.at[pl.ds(0, SIDE - 1)], strip_send),
    ):
        remote(piece, piece, sem, io_sem.at[0], at(0, 1)).wait_send()

    blocks = vir_back.at[pl.ds(0, SIDE - 1)]
    remote(blocks, blocks, swap_send.at[2], swap_recv.at[2], at(0, 1)).wait()
    for j in range(1, SIDE):
        for a in range(SIDE):
            vir_out[0, :, tile_of(a * sa + part_b[j])] = vir_back[j, :, a * TILE : (a + 1) * TILE]
    pair_occ.wait()
    for i in range(SIDE):
        for m in range(HALF):
            rows = rows_of(part_a[i] + (2 * m + 1 - par) * sb)
            occ_out[0, rows, :] = occ_back[(i * HALF + m) * ROWS : (i * HALF + m + 1) * ROWS]
    lines = shares.at[pl.ds(0, PLANE - 1)]
    remote(lines, lines, chi_send.at[0], chi_recv.at[0], at(0, 1)).wait()
    share = jnp.sum(shares[...], axis=0, keepdims=True) * scale
    share = fold(jnp.where(spot, jnp.broadcast_to(share, (RB, TILE)), 0.0))
    chi_out[...] = share[:, :RB]


def per_device(b_tensor, green_occ, green_vir, b_pattern, g_pattern):
    scale = -1.0 / (ORBS * math.sqrt(lax.axis_size("rep")))
    vmem = pl.BlockSpec(memory_space=pltpu.VMEM)
    hbm = pl.BlockSpec(memory_space=pltpu.HBM)
    dma = pltpu.SemaphoreType.DMA
    shapes = (
        jax.ShapeDtypeStruct((1, ORBS, TILE), BF16),
        jax.ShapeDtypeStruct((1, ROWS, ORBS * RB), BF16),
        jax.ShapeDtypeStruct((RB, RB), F32),
    )
    arguments = [
        pltpu.with_memory_space_constraint(t, pltpu.HBM)
        for t in (b_tensor, green_occ, green_vir, b_pattern, g_pattern)
    ]
    return pl.pallas_call(
        functools.partial(kernel, scale),
        out_shape=shapes,
        in_specs=[hbm] * 5,
        out_specs=(vmem, vmem, vmem),
        scratch_shapes=[
            pltpu.VMEM(b_tensor.shape, BF16),
            pltpu.VMEM(green_occ.shape, BF16),
            pltpu.VMEM(green_vir.shape, BF16),
            pltpu.SMEM(b_pattern.shape, jnp.int32),
            pltpu.SMEM(g_pattern.shape, jnp.int32),
            pltpu.VMEM((SIDE, ROWS, 128), BF16),
            pltpu.VMEM((SIDE, SIDE, ROWS, 128), BF16),
            pltpu.VMEM((SIDE, HALF, ROWS, ORBS), BF16),
            pltpu.VMEM((SIDE, SIDE, ROWS, WIDE), BF16),
            pltpu.VMEM((SIDE, 128, ORBS), BF16),
            pltpu.VMEM((SIDE, SIDE, ROWS, 2 * TILE), BF16),
            pltpu.VMEM((ORBS, 2 * TILE), BF16),
            pltpu.VMEM((WIDE, WIDE), BF16),
            pltpu.VMEM((128, WIDE), BF16),
            pltpu.VMEM((128, WIDE), BF16),
            pltpu.VMEM((2 * SIDE, 64, TILE), BF16),
            pltpu.VMEM((SIDE, ROWS, WIDE), BF16),
            pltpu.VMEM((512, 2 * TILE), BF16),
            pltpu.VMEM((512, TILE), BF16),
            pltpu.VMEM((512, TILE), BF16),
            pltpu.VMEM((PLANE, TILE), F32),
            pltpu.VMEM((SIDE, TILE), F32),
            dma((5,)),
            dma((2,)),
            dma((4,)),
            dma,
            dma((2,)),
            dma,
            dma((2, 7)),
            dma,
            dma((2, 3 * SUBS + SUBS // 2)),
            dma((4,)),
            dma((4,)),
            dma((2,)),
            dma((2,)),
        ],
        compiler_params=pltpu.CompilerParams(
            collective_id=0, has_side_effects=True, vmem_limit_bytes=40 * 1024 * 1024
        ),
        cost_estimate=pl.CostEstimate(flops=600_000_000, bytes_accessed=1_200_000, transcendentals=0),
    )(*arguments)


def solution(mesh):
    return jax.shard_map(
        per_device,
        mesh=mesh,
        in_specs=(
            P("rep", "grid", None),
            P("rep", "grid", None),
            P("rep", "grid", None),
            P("rep", None, None),
            P("rep", None, None),
        ),
        out_specs=(P("rep", None, "grid"), P("rep", "grid", None), P()),
        check_vma=False,
    )
```

```python
import functools
import math

import jax
import jax.numpy as jnp
from jax import lax
from jax.experimental import pallas as pl
from jax.experimental.pallas import tpu as pltpu
from jax.sharding import PartitionSpec as P

MESH = pl.DeviceIdType.MESH
SIDE = 8
PLANE = SIDE * SIDE
HALF = SIDE // 2
ROWS = 16
ORBS = 1024
RB = 8
TILE = ROWS * RB
WIDE = SIDE * TILE
F32 = jnp.float32
BF16 = jnp.bfloat16


def around(index, step):
    return lax.rem(index + (step + SIDE), SIDE)


FAR = [4, 5, 3, 6, 2, 7, 1]
ORDER = [0, 1, 7, 2, 6, 3, 5, 4]
SUBS = 4


def kernel(
    scale,
    b_hbm,
    occ_hbm,
    vir_hbm,
    bp_hbm,
    gp_hbm,
    occ_out,
    vir_out,
    chi_out,
    b_ref,
    occ_ref,
    vir_ref,
    bp_ref,
    gp_ref,
    vir_own,
    vir_all,
    occ_all,
    strips,
    left_side,
    landed,
    both,
    perm,
    mixed,
    merged,
    vir_land,
    vir_back,
    occ_pair,
    occ_two,
    occ_back,
    shares,
    shares_rep,
    io_sem,
    vir_send,
    vir_recv,
    occ_one_send,
    occ_one_recv,
    occ_ring_send,
    occ_ring_recv,
    strip_send,
    strip_recv,
    swap_send,
    swap_recv,
    chi_send,
    chi_recv,
):
    grid_ix = lax.axis_index("grid")
    rep_ix = lax.axis_index("rep")
    z, y = grid_ix // SIDE, grid_ix % SIDE
    core = rep_ix % 2
    a0 = z + core * (y - z)
    b0 = y + core * (z - y)
    sa = SIDE - (SIDE - 1) * core
    sb = 1 + (SIDE - 1) * core
    par = b0 % 2
    jb = b0 // 2
    mate = around(b0, 1 - 2 * par)
    abs_a = [around(a0, i) for i in range(SIDE)]
    abs_b = [around(b0, j) for j in range(SIDE)]
    part_a = [a * sa for a in abs_a]
    part_b = [b * sb for b in abs_b]

    def nat(i, j):
        return part_a[i % SIDE] + part_b[j % SIDE]

    def at(i, j):
        return (nat(i, j), rep_ix)

    def at_mate(i):
        return (part_a[i % SIDE] + mate * sb, rep_ix)

    def remote(src, dst, send, recv, where):
        return pltpu.make_async_remote_copy(
            src_ref=src, dst_ref=dst, send_sem=send, recv_sem=recv, device_id=where, device_id_type=MESH
        )

    def send(*copy):
        remote(*copy).start()

    def tile_of(i):
        return pl.ds(pl.multiple_of(i * TILE, TILE), TILE)

    def rows_of(i, count=ROWS):
        return pl.ds(pl.multiple_of(i * count, count), count)

    barrier = pltpu.get_barrier_semaphore()
    for i in range(1, SIDE):
        for where in (at(i, 0), at(0, i), (grid_ix, around(rep_ix, i))):
            pl.semaphore_signal(barrier, inc=1, device_id=where, device_id_type=MESH)

    loads = [
        pltpu.make_async_copy(src, dst, io_sem.at[i])
        for i, (src, dst) in enumerate(
            ((gp_hbm, gp_ref), (vir_hbm, vir_ref), (bp_hbm, bp_ref), (b_hbm, b_ref), (occ_hbm, occ_ref))
        )
    ]
    for load in loads:
        load.start()

    molecule = grid_ix // 4
    lane = lax.broadcasted_iota(jnp.int32, (ROWS, 128), 1)
    loads[0].wait()
    loads[1].wait()
    keeps = [
        jnp.where(lane < 64, gp_ref[0, molecule, 2 * t], gp_ref[0, molecule, 2 * t + 1]).astype(F32)
        for t in range(SIDE)
    ]
    tiles = [vir_ref[0, :, t * 128 : (t + 1) * 128].astype(F32) * keeps[t] for t in range(SIDE)]
    for bit in (1, 2, 4):
        high = (lane // ROWS // bit) % 2 + 2 * core
        for t in range(SIDE):
            if t & bit == 0:
                u = t + bit
                low_tile = jnp.where(high == 1, pltpu.roll(tiles[u], ROWS * bit, 1), tiles[t])
                high_tile = jnp.where(high == 0, pltpu.roll(tiles[t], 128 - ROWS * bit, 1), tiles[u])
                tiles[t], tiles[u] = low_tile, high_tile
    for b in range(SIDE):
        vir_own[b] = tiles[b].astype(BF16)
    vir_all[0, b0] = vir_own[b0]

    pl.semaphore_wait(barrier, 3 * (SIDE - 1))
    for j in FAR:
        send(vir_own.at[abs_b[j]], vir_all.at[0, b0], vir_send.at[0], vir_recv.at[0], at(0, j))
    loads[2].wait()
    loads[3].wait()
    for m in range(2 * SIDE):
        keep = jnp.full((ROWS, 512), bp_ref[0, molecule, m], jnp.int32).astype(F32).astype(BF16)
        cols = slice(m * 512, (m + 1) * 512)
        b_ref[0, :, cols] = b_ref[0, :, cols] * keep
    for i in range(SIDE):
        for b in range(SIDE):
            strips[0, i, :, b * TILE : (b + 1) * TILE] = b_ref[0, :, tile_of(part_a[i] + b * sb)]
    loads[4].wait()
    for t in range(SIDE):
        cols = slice(t * 128, (t + 1) * 128)
        occ_all[0, 0, :, cols] = occ_ref[0, :, cols] * keeps[t].astype(BF16)


    def strip_ring(way, d, u):
        sign = 1 - 2 * way
        send(
            strips.at[-sign * (d - 1) % SIDE, pl.ds(2 * u, 2)],
            strips.at[-sign * d % SIDE, pl.ds(2 * u, 2)],
            strip_send,
            strip_recv.at[way, SUBS * (d - 1) + u % (SUBS if d < 4 else SUBS // 2)],
            at(0, sign),
        )

    def strip_wait(way, d, u):
        piece = strips.at[(2 * way - 1) * d % SIDE, pl.ds(2 * u, 2)]
        slot = strip_recv.at[way, SUBS * (d - 1) + u % (SUBS if d < 4 else SUBS // 2)]
        remote(piece, piece, strip_send, slot, at(0, 1)).wait_recv()

    def occ_ring(way, d, g):
        sign = 1 - 2 * way
        send(
            occ_all.at[-sign * (d - 1) % SIDE, pl.ds(2 * g, 2)],
            occ_all.at[-sign * d % SIDE, pl.ds(2 * g, 2)],
            occ_ring_send,
            occ_ring_recv.at[way, 2 * (d - 1) + g if d < 4 else 6],
            at(sign, 0),
        )

    def occ_step(d):
        for g in range(2):
            for way in range(2):
                if d == 4 and g != way:
                    continue
                piece = occ_all.at[(2 * way - 1) * d % SIDE, pl.ds(2 * g, 2)]
                slot = occ_ring_recv.at[way, 2 * (d - 1) + g if d < 4 else 6]
                remote(piece, piece, occ_ring_send, slot, at(1, 0)).wait_recv()
                if d < 3 or (d == 3 and g == way):
                    occ_ring(way, d + 1, g)

    def swap(j):
        pair = pl.ds(pl.multiple_of(jb * 2 * TILE, 2 * TILE), 2 * TILE)
        for i in FAR:
            send(strips.at[j, i, :, pair], landed.at[-i % SIDE, j], swap_send.at[0], swap_recv.at[0], at(i, 0))
        landed[0, j] = strips[j, 0, :, pair]

    def fill(i, carry):
        target = lax.broadcasted_iota(jnp.int32, (256, WIDE), 1)
        target = (target % 128) * RB + target // 128
        row = lax.broadcasted_iota(jnp.int32, (256, WIDE), 0) + i * 256
        perm[pl.ds(pl.multiple_of(i * 256, 256), 256), :] = jnp.where(row == target, 1.0, 0.0).astype(BF16)
        return carry

    def part(j):
        apart = jnp.dot(strips[j].reshape(128, WIDE), perm[...], preferred_element_type=F32).astype(BF16)
        for i in range(SIDE):
            for q in range(RB):
                left_side[j, q * ROWS : (q + 1) * ROWS, i * 128 : (i + 1) * 128] = apart[
                    i * ROWS : (i + 1) * ROWS, q * 128 : (q + 1) * 128
                ]

    def contract(j):
        product = jnp.dot(left_side[j], vir_all[...].reshape(ORBS, 128), preferred_element_type=F32).astype(BF16)
        row = ORDER.index(j) * ROWS
        for q in range(RB):
            mixed[row : row + ROWS, q * 128 : (q + 1) * 128] = product[q * ROWS : (q + 1) * ROWS]

    def finish(*js):
        first = ORDER.index(js[0]) * ROWS
        rows = slice(first, first + len(js) * ROWS)
        merged[rows] = lax.dot_general(
            mixed[rows], perm[...], (((1,), (1,)), ((), ())), preferred_element_type=F32
        ).astype(BF16)
        for j in js:
            row = ORDER.index(j) * ROWS
            line = rows_of(abs_b[j] // 2)
            for i in FAR + [0]:
                piece = merged.at[row : row + ROWS, tile_of(abs_a[i])]
                land = vir_land.at[par * SIDE + -i % SIDE, line]
                if j % 2 == 1 or i != 0:
                    send(piece, land, swap_send.at[1], swap_recv.at[1], at_mate(i) if j % 2 else at(i, 0))
            if j % 2 == 0:
                vir_land[par * SIDE, line] = merged[row : row + ROWS, tile_of(a0)]
        for j in js:
            if j != 0:
                row = ORDER.index(j) * ROWS
                send(merged.at[row : row + ROWS], vir_back.at[-j % SIDE], swap_send.at[2], swap_recv.at[2], at(0, j))

    for m in (2, 1, 3):
        send(occ_all.at[0, 0], occ_all.at[0, -m % HALF], occ_one_send, occ_one_recv.at[-m % HALF // 2], at(0, 2 * m))
    for u in range(SUBS):
        for way in range(2):
            strip_ring(way, 1, u)
    swap(0)
    lax.fori_loop(0, WIDE // 256, fill, 0)

    blocks = vir_all.at[0, pl.ds(0, SIDE - 1)]
    remote(blocks, blocks, vir_send.at[0], vir_recv.at[0], at(0, 1)).wait()
    for d in (2, 1):
        for way in range(2):
            step = d * (1 - 2 * way)
            send(vir_all.at[0], vir_all.at[-step % SIDE], vir_send.at[1], vir_recv.at[1 if d == 1 else 2 + way], at(step, 0))

    def vir_relay():
        for way in range(2):
            sign = 1 - 2 * way
            chunk = vir_all.at[-2 * sign % SIDE]
            remote(chunk, chunk, vir_send.at[1], vir_recv.at[2 + way], at(1, 0)).wait_recv()
            half = pl.ds(way * HALF, HALF)
            send(
                vir_all.at[-2 * sign % SIDE, half],
                vir_all.at[HALF, half],
                vir_send.at[1],
                vir_recv.at[1],
                at(2 * sign, 0),
            )
            send(chunk, vir_all.at[-3 * sign % SIDE], vir_send.at[1], vir_recv.at[1], at(sign, 0))

    def occ_begin():
        for g in range(2):
            blocks = occ_all.at[0, pl.ds(2, 2)] if g else occ_all.at[0, pl.ds(1, 1)]
            remote(blocks, blocks, occ_one_send, occ_one_recv.at[g], at(0, 1)).wait_recv()
            for way in range(2):
                occ_ring(way, 1, g)

    def vir_end():
        chunks = vir_all.at[pl.ds(0, 5)]
        remote(chunks, chunks, vir_send.at[1], vir_recv.at[1], at(1, 0)).wait_recv()
        chunks = vir_all.at[pl.ds(0, SIDE - 1)]
        remote(chunks, chunks, vir_send.at[1], vir_recv.at[1], at(1, 0)).wait_send()

    def run(*steps):
        return [functools.partial(*step) for step in steps]

    work = {
        (1, 0): run((part, 0,)),
        (1, 2): run((occ_begin,)),
        (1, 3): run((vir_relay,)),
        (2, 0): run((swap, 1,), (swap, 7,)),
        (2, 1): run((part, 1,)),
        (2, 2): run((part, 7,)),
        (2, 3): run((occ_step, 1,)),
        (3, 0): run((swap, 2,), (swap, 6,)),
        (3, 1): run((part, 2,), (vir_end,), (contract, 0,), (contract, 1,)),
        (3, 2): run((part, 6,), (contract, 7,), (contract, 2,), (contract, 6,)),
        (3, 3): run((occ_step, 2,), (finish, 0, 1, 7, 2, 6,)),
        (4, 0): run((swap, 3,), (swap, 5,), (part, 3,), (contract, 3,)),
        (4, 1): run((part, 5,), (contract, 5,), (finish, 3, 5,)),
    }
    for d in range(1, 5):
        for u in range(SUBS if d < 4 else SUBS // 2):
            for way in range(2):
                sub = u if d < 4 else u + way * SUBS // 2
                strip_wait(way, d, sub)
                if d < 3 or (d == 3 and u // (SUBS // 2) == way):
                    strip_ring(way, d + 1, sub)
            for step in work.get((d, u), ()):
                step()
    swap(4)
    part(4)
    contract(4)

    finish(4)
    occ_step(3)
    pieces = landed.at[pl.ds(0, SIDE - 1)]
    remote(pieces, pieces, swap_send.at[0], swap_recv.at[0], at(1, 0)).wait()
    for i in range(SIDE):
        for j in range(SIDE):
            both[rows_of(nat(i, j)), :] = landed[i, j]

    turn = [lax.rem(jb + m, HALF) for m in range(HALF)]

    def put_occ(i):
        product = jnp.dot(occ_all[i].reshape(64, ORBS), both[...], preferred_element_type=F32).astype(BF16)
        for m in range(HALF):
            occ_pair[rows_of(i * HALF + turn[m]), :] = product[m * ROWS : (m + 1) * ROWS]

    for i in (0, 1, 7, 2, 6, 3, 5):
        put_occ(i)
    occ_step(4)
    put_occ(4)
    occ_two[...] = occ_pair[:, tile_of(1 - par)]

    most = vir_land.at[pl.ds(0, 2 * SIDE - 1)]
    remote(most, most, swap_send.at[1], swap_recv.at[1], at(1, 0)).wait()

    gram = jnp.zeros((TILE, TILE), F32)
    for c in range(2):
        mine = occ_pair[:, c * TILE : (c + 1) * TILE]
        theirs = vir_land[c * SIDE : (c + 1) * SIDE].reshape(512, TILE)
        gram += lax.dot_general(mine, theirs, (((0,), (0,)), ((), ())), preferred_element_type=F32)
    row = lax.broadcasted_iota(jnp.int32, (TILE, TILE), 0)
    col = lax.broadcasted_iota(jnp.int32, (TILE, TILE), 1)
    gram = jnp.where(row // RB == col // RB, gram, 0.0)
    share = jnp.sum(gram.reshape(ROWS, RB, TILE), axis=0)

    def fold(values):
        for shift in (8, 16, 32, 64):
            values = values + pltpu.roll(values, shift, 1)
        return values

    spot = lax.broadcasted_iota(jnp.int32, (RB, TILE), 1) // RB == lax.broadcasted_iota(jnp.int32, (RB, TILE), 0)
    share = jnp.sum(jnp.where(spot, fold(share), 0.0), axis=0, keepdims=True)
    shares_rep[pl.ds(rep_ix, 1), :] = share
    line = shares_rep.at[pl.ds(rep_ix, 1)]
    for i in range(1, SIDE):
        send(line, line, chi_send.at[1], chi_recv.at[1], (grid_ix, around(rep_ix, i)))

    pair_occ = remote(occ_two, occ_back, swap_send.at[3], swap_recv.at[3], at_mate(0))

    lines = shares_rep.at[pl.ds(0, SIDE - 1)]
    remote(lines, lines, chi_send.at[1], chi_recv.at[1], (grid_ix, around(rep_ix, 1))).wait()
    shares[pl.ds(grid_ix, 1), :] = jnp.sum(shares_rep[...], axis=0, keepdims=True)
    line = shares.at[pl.ds(grid_ix, 1)]
    for i in FAR + [0]:
        for j in FAR + [0]:
            if (i, j) != (0, 0):
                send(line, line, chi_send.at[0], chi_recv.at[0], at(i, j))
    pair_occ.start()

    for a in range(SIDE):
        vir_out[0, :, tile_of(a * sa + part_b[0])] = merged[:ROWS, a * TILE : (a + 1) * TILE]
    for i in range(SIDE):
        for m in range(HALF):
            rows = rows_of(part_a[i] + (2 * m + par) * sb)
            occ_out[0, rows, :] = occ_pair[(i * HALF + m) * ROWS : (i * HALF + m + 1) * ROWS, tile_of(par)]
    for piece, sem in (
        (occ_all.at[0, pl.ds(0, HALF - 1)], occ_one_send),
        (occ_all.at[pl.ds(0, SIDE - 1)], occ_ring_send),
        (strips.at[pl.ds(0, SIDE - 1)], strip_send),
    ):
        remote(piece, piece, sem, io_sem.at[0], at(0, 1)).wait_send()

    blocks = vir_back.at[pl.ds(0, SIDE - 1)]
    remote(blocks, blocks, swap_send.at[2], swap_recv.at[2], at(0, 1)).wait()
    for j in range(1, SIDE):
        for a in range(SIDE):
            vir_out[0, :, tile_of(a * sa + part_b[j])] = vir_back[j, :, a * TILE : (a + 1) * TILE]
    pair_occ.wait()
    for i in range(SIDE):
        for m in range(HALF):
            rows = rows_of(part_a[i] + (2 * m + 1 - par) * sb)
            occ_out[0, rows, :] = occ_back[(i * HALF + m) * ROWS : (i * HALF + m + 1) * ROWS]
    lines = shares.at[pl.ds(0, PLANE - 1)]
    remote(lines, lines, chi_send.at[0], chi_recv.at[0], at(0, 1)).wait()
    share = jnp.sum(shares[...], axis=0, keepdims=True) * scale
    share = fold(jnp.where(spot, jnp.broadcast_to(share, (RB, TILE)), 0.0))
    chi_out[...] = share[:, :RB]


def per_device(b_tensor, green_occ, green_vir, b_pattern, g_pattern):
    scale = -1.0 / (ORBS * math.sqrt(lax.axis_size("rep")))
    vmem = pl.BlockSpec(memory_space=pltpu.VMEM)
    hbm = pl.BlockSpec(memory_space=pltpu.HBM)
    dma = pltpu.SemaphoreType.DMA
    shapes = (
        jax.ShapeDtypeStruct((1, ORBS, TILE), BF16),
        jax.ShapeDtypeStruct((1, ROWS, ORBS * RB), BF16),
        jax.ShapeDtypeStruct((RB, RB), F32),
    )
    arguments = [
        pltpu.with_memory_space_constraint(t, pltpu.HBM)
        for t in (b_tensor, green_occ, green_vir, b_pattern, g_pattern)
    ]
    return pl.pallas_call(
        functools.partial(kernel, scale),
        out_shape=shapes,
        in_specs=[hbm] * 5,
        out_specs=(vmem, vmem, vmem),
        scratch_shapes=[
            pltpu.VMEM(b_tensor.shape, BF16),
            pltpu.VMEM(green_occ.shape, BF16),
            pltpu.VMEM(green_vir.shape, BF16),
            pltpu.SMEM(b_pattern.shape, jnp.int32),
            pltpu.SMEM(g_pattern.shape, jnp.int32),
            pltpu.VMEM((SIDE, ROWS, 128), BF16),
            pltpu.VMEM((SIDE, SIDE, ROWS, 128), BF16),
            pltpu.VMEM((SIDE, HALF, ROWS, ORBS), BF16),
            pltpu.VMEM((SIDE, SIDE, ROWS, WIDE), BF16),
            pltpu.VMEM((SIDE, 128, ORBS), BF16),
            pltpu.VMEM((SIDE, SIDE, ROWS, 2 * TILE), BF16),
            pltpu.VMEM((ORBS, 2 * TILE), BF16),
            pltpu.VMEM((WIDE, WIDE), BF16),
            pltpu.VMEM((128, WIDE), BF16),
            pltpu.VMEM((128, WIDE), BF16),
            pltpu.VMEM((2 * SIDE, 64, TILE), BF16),
            pltpu.VMEM((SIDE, ROWS, WIDE), BF16),
            pltpu.VMEM((512, 2 * TILE), BF16),
            pltpu.VMEM((512, TILE), BF16),
            pltpu.VMEM((512, TILE), BF16),
            pltpu.VMEM((PLANE, TILE), F32),
            pltpu.VMEM((SIDE, TILE), F32),
            dma((5,)),
            dma((2,)),
            dma((4,)),
            dma,
            dma((2,)),
            dma,
            dma((2, 7)),
            dma,
            dma((2, 3 * SUBS + SUBS // 2)),
            dma((4,)),
            dma((4,)),
            dma((2,)),
            dma((2,)),
        ],
        compiler_params=pltpu.CompilerParams(
            collective_id=0, has_side_effects=True, vmem_limit_bytes=40 * 1024 * 1024
        ),
        cost_estimate=pl.CostEstimate(flops=600_000_000, bytes_accessed=1_200_000, transcendentals=0),
    )(*arguments)


def solution(mesh):
    return jax.shard_map(
        per_device,
        mesh=mesh,
        in_specs=(
            P("rep", "grid", None),
            P("rep", "grid", None),
            P("rep", "grid", None),
            P("rep", None, None),
            P("rep", None, None),
        ),
        out_specs=(P("rep", None, "grid"), P("rep", "grid", None), P()),
        check_vma=False,
    )
```
